512 devices in a mesh: trace: 8 (over y), seq: 64 (over z, x, core).
Axes of the slice: x: 4, y: 8, z: 8, core: 2. Of those that a mesh axis runs over, the one named last changes fastest.
Arguments:
- sel_hidden: bfloat16 [8, 512, 8, 4096], P('trace', 'seq'), may hold values from -6 to 6
- w_qkv: bfloat16 [4096, 3072], P('seq', 'trace'), may hold values from -0.09375 to 0.09375
- cache_pool: bfloat16 [8, 65536, 1024], P('trace', 'seq'), may hold values from -6 to 6
- block_owner: int32 [8, 512], P(None, 'seq'), may hold values from 0 to 63, as said below
- doc_lengths: int32 [8, 32], replicated, may hold values from 1 to 32, 512 in all within a row
- sel_index: int32 [8, 512, 8], P('trace', 'seq'), may hold values from 0 to 127, as said below
- sel_count: int32 [8, 512], P('trace', 'seq'), may hold values from 4 to 8, as said below
Outputs:
- attended: bfloat16 [8, 512, 8, 2048], P('trace', 'seq')
- blended: bfloat16 [8, 65536, 1024], P('trace', 'seq')
The draws below stay inside these ranges and needn't reach their ends.
Inputs may be any that keep to these rules, and one draw needn't show every extreme that they name: `block_owner`: for each index of seq, the entries of all traces' blocks held there name each of the 64 cached slots held at that index once; one owner serves at most 2 blocks of one shard, and exactly 2 to some shard at every index. `sel_index`: within each block the 8 offsets are distinct and rising. `sel_count`: some block of every trace has all 8 slots live. `doc_lengths`: lengths of one trace sum to 512.
All inputs are finite; a program needn't handle non-finite values.
Results may differ from the reference program's by a relative error of at most 0.015.
Values may be sent and summed in bfloat16 or wider, within the bound.
No kernel may reach another device: no remote copies, remote signals or barrier semaphores. Data moves between devices by JAX's collectives and lax.ppermute only.
A program may use at most 64 MiB of HBM per device.

```python
import math
import jax
import jax.numpy as jnp
import numpy as np
from jax import lax

D = 4096
QUERY_HEADS = 16
KEY_VALUE_HEADS = 4
HEAD_SIZE = 128
WINDOW_TOKENS = 2048
BLOCK_TOKENS = 128
RECOMPUTE_SLOTS = 8
BLK_DEV = 8
TRACE_COUNT = 8
TRACE_BLOCKS = 512
SHARD_TOKENS = 1024
SEQ_LEN = 65536
CAP = 2
NDOC = 32
DOC_MOST = 32
QKV = 3072
KVW = 1024
N_SEQ = 64


def owner_layout(seq_key):
    key_order, key_shift, key_label = jax.random.split(seq_key, 3)
    group_count = (BLK_DEV + CAP - 1) // CAP
    order = jax.random.permutation(key_order, BLK_DEV).astype(jnp.int32)
    shifts = jax.random.permutation(key_shift, TRACE_COUNT)[:group_count].astype(jnp.int32)
    relabel = jax.random.permutation(key_label, TRACE_COUNT).astype(jnp.int32)
    inverse = jnp.argsort(relabel, stable=True).astype(jnp.int32)
    trace_col = jnp.arange(TRACE_COUNT, dtype=jnp.int32)[:, None]
    group_of = order[None, :] // CAP
    owner = relabel[(inverse[trace_col] + shifts[group_of]) % TRACE_COUNT]
    return (owner * BLK_DEV + order[None, :]).astype(jnp.int32)


def draw_block_owner(key, part):
    layouts = jax.vmap(owner_layout)(jax.random.split(key, N_SEQ))
    return jnp.transpose(layouts, (1, 0, 2)).reshape(TRACE_COUNT, N_SEQ * BLK_DEV).astype(jnp.int32)


def block_offsets(block_key):
    return jax.random.permutation(block_key, BLOCK_TOKENS).astype(jnp.int32)


def draw_sel_index(key, part):
    block_keys = jax.random.split(key, TRACE_COUNT * TRACE_BLOCKS)
    shuffled = jax.vmap(block_offsets)(block_keys)
    picked = jnp.sort(shuffled[:, :RECOMPUTE_SLOTS], axis=1)
    return picked.reshape(TRACE_COUNT, TRACE_BLOCKS, RECOMPUTE_SLOTS).astype(jnp.int32)


def draw_sel_count(key, part):
    key_counts, key_fullest = jax.random.split(key)
    counts = jax.random.randint(key_counts, (TRACE_COUNT, TRACE_BLOCKS), RECOMPUTE_SLOTS // 2, RECOMPUTE_SLOTS + 1)
    fullest = jax.random.randint(key_fullest, (TRACE_COUNT,), 0, TRACE_BLOCKS)
    counts = jnp.where(jnp.arange(TRACE_BLOCKS)[None, :] == fullest[:, None], RECOMPUTE_SLOTS, counts)
    return counts.astype(jnp.int32)


def level_of(stream_key, shape, cuts, smallest, top_value):
    factor_of, own = 1.0, jax.random.fold_in(stream_key, 6)
    for dim, parts in cuts:
        heights = jnp.exp(jax.random.uniform(jax.random.fold_in(own, dim), (parts,), jnp.float32, smallest / len(cuts), top_value / len(cuts)))
        factor_of = factor_of * jnp.repeat(heights, shape[dim] // parts).reshape([-1 if axis == dim else 1 for axis in range(len(shape))])
    return factor_of


def split_up(count, total, reach, skew):
    weights = [(1 << 20) // math.isqrt(grade ** skew) + 1 for grade in range(2, count + 1)]
    surplus, holding = total - reach - (count - 1), [1] * (count - 1)
    while surplus > 0:
        free = [i for i in range(count - 1) if holding[i] < reach]
        pool, budget = sum([weights[i] for i in free]), surplus
        for i in free:
            extra = min(reach - holding[i], max(1, budget * weights[i] // pool), surplus)
            holding[i] = holding[i] + extra
            surplus = surplus - extra
    return np.array([reach] + holding)


def ragged(rng, amount, total, most, slope):
    if amount == 2:
        one = jax.random.randint(rng, (), max(1, total - most), min(most, total - 1) + 1)
        return jnp.stack([one, total - one])
    tallies = jnp.asarray(split_up(amount, total, most, slope), jnp.int32)
    pairs = (amount - 1) // 2
    giver, taker = tallies[1:1 + 2 * pairs:2], tallies[2:2 + 2 * pairs:2]
    room = jnp.minimum(giver - 1, most - taker)
    moved = jax.random.randint(jax.random.fold_in(rng, 1), (pairs,), 0, 1 << 20) % (room + 1)
    tallies = tallies.at[1:1 + 2 * pairs:2].set(giver - moved).at[2:2 + 2 * pairs:2].set(taker + moved)
    return tallies[jax.random.permutation(jax.random.fold_in(rng, 2), amount)]


def normal_values(rng, extent, width, most, pieces=(), kind=jnp.bfloat16):
    result = jax.random.normal(rng, extent, jnp.float32) * width
    if len(pieces) > 0:
        result = level_of(rng, extent, pieces, -0.22, 0.18) * result
    return jnp.clip(result, min=-most, max=most).astype(kind)


def setup_inputs(seed: int = 0) -> dict:
    keys = jax.random.split(jax.random.key(seed), 8)
    return {
        "sel_hidden": normal_values(keys[0], (TRACE_COUNT, TRACE_BLOCKS, RECOMPUTE_SLOTS, D), 1.0, 6.0, ((0, 8), (1, 64))),
        "w_qkv": normal_values(keys[1], (D, QKV), D ** -0.5, 0.09375, ((0, 64), (1, 8))),
        "cache_pool": normal_values(keys[2], (TRACE_COUNT, SEQ_LEN, KVW), 1.0, 6.0, ((0, 8), (1, 64))),
        "block_owner": draw_block_owner(jax.random.fold_in(keys[7], 71), 0),
        "doc_lengths": jax.vmap(lambda own: ragged(own, NDOC, TRACE_BLOCKS, DOC_MOST, 2))(jax.random.split(keys[4], TRACE_COUNT)).reshape((TRACE_COUNT, NDOC)).astype(jnp.int32),
        "sel_index": draw_sel_index(jax.random.fold_in(keys[7], 71), 0),
        "sel_count": draw_sel_count(jax.random.fold_in(keys[7], 71), 0),
    }


ROPE_BASE = 10000.0


def apply_rotary(values, token_positions):
    half_width = values.shape[-1] // 2
    frequency = 1.0 / (ROPE_BASE ** (jnp.arange(half_width, dtype=jnp.float32) * 2.0 / values.shape[-1]))
    angles = token_positions.astype(jnp.float32)[..., None, None] * frequency
    cos_part = jnp.cos(angles)
    sin_part = jnp.sin(angles)
    values = values.astype(jnp.float32)
    low_half = values[..., :half_width]
    high_half = values[..., half_width:]
    return jnp.concatenate([low_half * cos_part - high_half * sin_part, high_half * cos_part + low_half * sin_part], axis=-1)


def reference(sel_hidden, w_qkv, cache_pool, block_owner, doc_lengths, sel_index, sel_count):
    all_rows = TRACE_COUNT * TRACE_BLOCKS * RECOMPUTE_SLOTS
    query_columns = QUERY_HEADS * HEAD_SIZE
    key_columns = KEY_VALUE_HEADS * HEAD_SIZE
    head_groups = QUERY_HEADS // KEY_VALUE_HEADS
    merged_rows = jnp.dot(sel_hidden.reshape(all_rows, D), w_qkv, preferred_element_type=jnp.float32).astype(jnp.bfloat16)
    merged_rows = lax.optimization_barrier(merged_rows)
    block_row = jnp.arange(TRACE_BLOCKS, dtype=jnp.int32)
    token_positions = (block_row[None, :, None] * BLOCK_TOKENS + sel_index).astype(jnp.int32)
    is_live = jnp.arange(RECOMPUTE_SLOTS, dtype=jnp.int32)[None, None, :] < sel_count[:, :, None]
    query_rows = apply_rotary(merged_rows[:, :query_columns].reshape(TRACE_COUNT, TRACE_BLOCKS, RECOMPUTE_SLOTS, QUERY_HEADS, HEAD_SIZE), token_positions).astype(jnp.bfloat16)
    query_rows = lax.optimization_barrier(query_rows)
    recomputed_keys = apply_rotary(merged_rows[:, query_columns:query_columns + key_columns].reshape(TRACE_COUNT, TRACE_BLOCKS, RECOMPUTE_SLOTS, KEY_VALUE_HEADS, HEAD_SIZE), token_positions).astype(jnp.bfloat16)
    fresh_rows = jnp.concatenate([recomputed_keys.reshape(TRACE_COUNT, TRACE_BLOCKS, RECOMPUTE_SLOTS, key_columns), merged_rows[:, query_columns + key_columns:].reshape(TRACE_COUNT, TRACE_BLOCKS, RECOMPUTE_SLOTS, key_columns)], axis=-1)
    owner_of = (block_owner // BLK_DEV).astype(jnp.int32)
    source_block = ((block_row // BLK_DEV)[None, :] * BLK_DEV + block_owner % BLK_DEV).astype(jnp.int32)
    pool_blocks = cache_pool.reshape(TRACE_COUNT, TRACE_BLOCKS, BLOCK_TOKENS, KVW)
    cached_values = pool_blocks[owner_of, source_block]
    doc_ends = jnp.cumsum(doc_lengths, axis=1)
    start_block = jnp.sum(jnp.where(doc_ends[:, None, :] <= block_row[None, :, None], doc_lengths[:, None, :], 0), axis=-1)
    token_offset = jnp.broadcast_to((start_block * BLOCK_TOKENS).astype(jnp.int32)[:, :, None], (TRACE_COUNT, TRACE_BLOCKS, BLOCK_TOKENS))

    def blend_trace(inputs):
        cached_transposed, shift_transposed, index_t, live_t, fresh_t = inputs
        cached_transposed = cached_transposed.astype(jnp.float32)
        keys_transposed = apply_rotary(cached_transposed[..., :key_columns].reshape(TRACE_BLOCKS, BLOCK_TOKENS, KEY_VALUE_HEADS, HEAD_SIZE), shift_transposed).reshape(TRACE_BLOCKS, BLOCK_TOKENS, key_columns)
        restored = jnp.concatenate([keys_transposed, cached_transposed[..., key_columns:]], axis=-1)
        slot_hits = (index_t[..., None] == jnp.arange(BLOCK_TOKENS, dtype=jnp.int32)) & live_t[..., None]
        placed = jnp.einsum('bsp,bsx->bpx', slot_hits.astype(jnp.float32), fresh_t.astype(jnp.float32), precision=lax.Precision.HIGHEST)
        chosen = jnp.any(slot_hits, axis=1)
        return jnp.where(chosen[..., None], placed, restored).astype(jnp.bfloat16)

    blended = lax.map(blend_trace, (cached_values, token_offset, sel_index, is_live, fresh_rows))
    blended = lax.optimization_barrier(blended.reshape(TRACE_COUNT, SEQ_LEN, KVW))
    padded = jnp.pad(blended, ((0, 0), (WINDOW_TOKENS, 0), (0, 0)))
    sequence_rows = BLK_DEV * RECOMPUTE_SLOTS
    query_sets = query_rows.reshape(TRACE_COUNT, N_SEQ, sequence_rows, QUERY_HEADS, HEAD_SIZE)
    pos_sets = token_positions.reshape(TRACE_COUNT, N_SEQ, sequence_rows)

    def one_shard(flat_index):
        trace_at = (flat_index // N_SEQ).astype(jnp.int32)
        shard_at = (flat_index % N_SEQ).astype(jnp.int32)
        trace_keys = lax.dynamic_index_in_dim(padded, trace_at, 0, keepdims=False)
        window_key_rows = lax.dynamic_slice_in_dim(trace_keys, (shard_at * SHARD_TOKENS).astype(jnp.int32), WINDOW_TOKENS + SHARD_TOKENS, 0)
        key_pos = (shard_at * SHARD_TOKENS - WINDOW_TOKENS + jnp.arange(WINDOW_TOKENS + SHARD_TOKENS, dtype=jnp.int32)).astype(jnp.int32)
        shard_query_rows = lax.dynamic_index_in_dim(lax.dynamic_index_in_dim(query_sets, trace_at, 0, keepdims=False), shard_at, 0, keepdims=False)
        shard_pos = lax.dynamic_index_in_dim(lax.dynamic_index_in_dim(pos_sets, trace_at, 0, keepdims=False), shard_at, 0, keepdims=False)
        key_head_split = window_key_rows[:, :key_columns].reshape(WINDOW_TOKENS + SHARD_TOKENS, KEY_VALUE_HEADS, HEAD_SIZE).astype(jnp.float32)
        value_head_split = window_key_rows[:, key_columns:].reshape(WINDOW_TOKENS + SHARD_TOKENS, KEY_VALUE_HEADS, HEAD_SIZE).astype(jnp.float32)
        query_head_split = shard_query_rows.reshape(sequence_rows, KEY_VALUE_HEADS, head_groups, HEAD_SIZE).astype(jnp.float32)
        scores = jnp.einsum('rkgd,nkd->kgrn', query_head_split, key_head_split) * (HEAD_SIZE ** -0.5)
        allowed = (key_pos[None, :] <= shard_pos[:, None]) & (key_pos[None, :] > shard_pos[:, None] - WINDOW_TOKENS) & (key_pos[None, :] >= 0)
        weights = jnp.where(allowed[None, None], jnp.exp(scores), 0.0)
        denominator = jnp.sum(weights, axis=-1)
        rounded = lax.optimization_barrier(weights.astype(jnp.bfloat16)).astype(jnp.float32)
        numerator = jnp.einsum('kgrn,nkd->rkgd', rounded, value_head_split)
        layer_output = numerator / jnp.transpose(denominator, (2, 0, 1))[..., None]
        return layer_output.reshape(sequence_rows, QUERY_HEADS * HEAD_SIZE)

    outputs = lax.map(one_shard, jnp.arange(TRACE_COUNT * N_SEQ, dtype=jnp.int32))
    outputs = outputs.reshape(TRACE_COUNT, TRACE_BLOCKS, RECOMPUTE_SLOTS, QUERY_HEADS * HEAD_SIZE)
    attended = jnp.where(is_live[..., None], outputs, 0.0).astype(jnp.bfloat16)
    return attended, blended
```

```python
import jax
import jax.numpy as jnp
from jax import lax
from jax.experimental import pallas as pl
from jax.experimental.pallas import tpu as pltpu
from jax.sharding import Mesh
from jax.sharding import PartitionSpec as P

QH = 16
KH = 4
HD = 128
GROUP = QH // KH
WINDOW = 2048
BASE = 10000.0
NX, NC = 4, 2
CAP = 2
SEQ = ("z", "x", "c")
XC = ("x", "c")
F32 = jnp.float32
BF = jnp.bfloat16
VM = pl.BlockSpec(memory_space=pltpu.VMEM)
SM = pl.BlockSpec(memory_space=pltpu.SMEM)
ANY = pl.BlockSpec(memory_space=pl.ANY)


def call(kernel, out, ins, outs, scratch=(), flops=0, moved=0, vmem=48):
    return pl.pallas_call(
        kernel,
        out_shape=out,
        in_specs=ins,
        out_specs=outs,
        scratch_shapes=list(scratch),
        compiler_params=pltpu.CompilerParams(vmem_limit_bytes=vmem << 20),
        cost_estimate=pl.CostEstimate(flops=flops, bytes_accessed=moved, transcendentals=0),
    )


def pick_kernel(owner, me, pool, out, sem):
    blocks = owner.shape[1]
    rows = pool.shape[0] // blocks
    mine = me[0]
    for t in range(owner.shape[0]):
        count = jnp.int32(0)
        for b in range(blocks):
            o = owner[t, b]
            slot = o % blocks
            hit = o // blocks == mine

            @pl.when(hit)
            def _(slot=slot, count=count):
                start = pl.multiple_of(slot * rows, rows)
                pltpu.make_async_copy(
                    pool.at[pl.ds(start, rows)], out.at[t * CAP + count], sem.at[slot]
                ).start()

            count = count + hit.astype(jnp.int32)
    for slot in range(blocks):
        pltpu.make_async_copy(pool.at[pl.ds(slot * rows, rows)], out.at[0], sem.at[slot]).wait()


def head(ref, n):
    return ref[n // 3, :, pl.ds((n % 3) * HD, HD)]


def rotated(x, cos, sin):
    x = x.astype(F32)
    return x * cos + pltpu.roll(x, HD // 2, 1) * sin


def rope_kernel(proj, cos, sin, sel, q_out, fresh):
    for n in range(QH):
        q_out[:, n * HD : (n + 1) * HD] = rotated(head(proj, n), cos[...], sin[...]).astype(BF)
    rows = q_out.shape[0]
    q_out[:, QH * HD :] = jnp.broadcast_to(sel[...].astype(F32), (rows, HD)).astype(BF)
    for n in range(KH):
        k = rotated(head(proj, QH + n), cos[...], sin[...])
        fresh[:, n * HD : (n + 1) * HD] = k.astype(BF)
        fresh[:, (KH + n) * HD : (KH + n + 1) * HD] = head(proj, QH + KH + n)


def blend_kernel(
    owner, me, spots, kcos, ksin, fresh, q0, q1, q2, incoming,
    blended, num0, den0, p1, p2, kv, qs, sem, out_sem,
):
    blocks = owner.shape[1]
    tokens, width = kv.shape
    rows = tokens // blocks
    mine = me[0]
    own = [owner[mine, b] // blocks for b in range(blocks)]
    for b in range(blocks):
        rank = jnp.int32(0)
        for e in range(b):
            rank = rank + (own[e] == own[b]).astype(jnp.int32)
        pltpu.make_async_copy(
            incoming.at[own[b] * CAP + rank], kv.at[pl.ds(b * rows, rows)], sem.at[b]
        ).start()
    n_q = q0.shape[0]
    for k in range(KH):
        for i, q in enumerate((q0, q1, q2)):
            for g in range(GROUP):
                h = k * GROUP + g
                qs[k, pl.ds((i * GROUP + g) * n_q, n_q), :] = q[:, h * HD : (h + 1) * HD]
    ones = jnp.ones((n_q, HD), BF)
    for b in range(blocks):
        at = lax.broadcasted_iota(jnp.int32, (rows, n_q), 0) + b * rows
        hits = (at == spots[...]).astype(F32).astype(BF)
        chosen = jnp.dot(hits, ones, preferred_element_type=F32) > 0.5
        here = pl.ds(b * rows, rows)
        pltpu.make_async_copy(incoming.at[0], kv.at[here], sem.at[b]).wait()
        cos, sin = kcos[b : b + 1, :], ksin[b : b + 1, :]
        for n in range(2 * KH):
            cols = pl.ds(n * HD, HD)
            x = kv[here, cols]
            x = rotated(x, cos, sin) if n < KH else x.astype(F32)
            placed = jnp.dot(hits, fresh[:, cols], preferred_element_type=F32)
            kv[here, cols] = jnp.where(chosen, placed, x).astype(BF)
        pltpu.make_async_copy(kv.at[here], blended.at[here], out_sem.at[b]).start()

    spot_row = lax.broadcasted_iota(jnp.int32, (n_q, 1), 0) // 8 * rows

    def where_of(q):
        return spot_row + q[:, QH * HD : QH * HD + 1].astype(F32).astype(jnp.int32)

    key = lax.broadcasted_iota(jnp.int32, (n_q, tokens), 1)
    ok0 = key <= where_of(q0)
    ok2 = key > where_of(q2)
    lane = lax.broadcasted_iota(jnp.int32, (n_q, HD), 1)
    dens = [jnp.zeros((n_q, HD), F32) for _ in range(3)]
    for k in range(KH):
        keys = kv[:, k * HD : (k + 1) * HD]
        values = kv[:, (KH + k) * HD : (KH + k + 1) * HD]
        for i in range(3):
            part = qs[k, pl.ds(i * GROUP * n_q, GROUP * n_q), :]
            scores = lax.dot_general(
                part, keys, (((1,), (1,)), ((), ())), preferred_element_type=F32
            )
            w = jnp.exp(scores * HD ** (-0.5))
            if i != 1:
                w = jnp.where(
                    (ok0 if i == 0 else ok2)[None], w.reshape(GROUP, n_q, tokens), 0.0
                ).reshape(GROUP * n_q, tokens)
            total = jnp.sum(w, axis=1, keepdims=True)
            num = jnp.dot(w.astype(BF), values, preferred_element_type=F32)
            for g in range(GROUP):
                h = k * GROUP + g
                here = slice(g * n_q, (g + 1) * n_q)
                dens[i] = jnp.where(lane == h, total[here], dens[i])
                cols = pl.ds(h * HD, HD)
                if i == 0:
                    num0[:, cols] = num[here]
                elif i == 1:
                    p1[:, cols] = num[here].astype(BF)
                else:
                    p2[:, cols] = num[here].astype(BF)
    den0[...] = dens[0]
    for p, d in ((p1, dens[1]), (p2, dens[2])):
        high = d.astype(BF)
        low = d - high.astype(F32)
        p[:, QH * HD :] = jnp.where(
            lane < QH, high.astype(F32), pltpu.roll(low, QH, 1)
        ).astype(BF)
    for b in range(blocks):
        here = pl.ds(b * rows, rows)
        pltpu.make_async_copy(kv.at[here], blended.at[here], out_sem.at[b]).wait()


def merge_kernel(num0, den0, r1, r2, live, out):
    total = den0[...]
    for r in (r1, r2):
        d = r[:, QH * HD :].astype(F32)
        total = total + d + pltpu.roll(d, HD - QH, 1)
    alive = live[...] > 0
    for h in range(QH):
        cols = pl.ds(h * HD, HD)
        num = num0[:, cols] + r1[:, cols].astype(F32) + r2[:, cols].astype(F32)
        out[:, cols] = jnp.where(alive, num / total[:, h : h + 1], 0.0).astype(BF)


def half_turns(angles):
    cos, sin = jnp.cos(angles), jnp.sin(angles)
    return jnp.concatenate([cos, cos], -1), jnp.concatenate([-sin, sin], -1)


def on_device(sel_hidden, w_qkv, cache_pool, block_owner, doc_lengths, sel_index, sel_count):
    ny, nz = lax.axis_size("y"), lax.axis_size("z")
    y = lax.axis_index("y")
    shard = lax.axis_index(SEQ)
    group = NX * NC
    n_seq = nz * group
    _, blocks, slots, d = sel_hidden.shape
    rows = blocks * slots
    tokens, kvw = cache_pool.shape[1:]
    block_len = tokens // blocks
    cols = w_qkv.shape[1]
    me = y.reshape(1).astype(jnp.int32)

    outgoing = call(
        pick_kernel,
        jax.ShapeDtypeStruct((ny * CAP, block_len, kvw), BF),
        [SM, SM, ANY], ANY,
        [pltpu.SemaphoreType.DMA((blocks,))],
        moved=4 * tokens * kvw,
    )(block_owner, me, cache_pool[0])
    incoming = lax.all_to_all(outgoing, "y", 0, 0, tiled=True)

    flip = [(a * group + b, b * group + a) for a in range(ny) for b in range(group)]
    far = [(a * group + b, (b ^ 4) * group + a) for a in range(ny) for b in range(group)]
    over = ("y", "x", "c")
    w = (lax.ppermute(w_qkv, over, flip), lax.ppermute(w_qkv, over, far))

    def paired(mine, other, bit, axis):
        low = (y // bit) % 2 == 0
        return jnp.stack([jnp.where(low, mine, other), jnp.where(low, other, mine)], axis)

    w = paired(w[0], w[1], 4, 0)
    for axis, bit in ((1, 2), (2, 1)):
        other = lax.ppermute(w, "y", [(i, i ^ bit) for i in range(ny)])
        w = paired(w, other, bit, axis)
    w = lax.all_gather(w.reshape(-1, cols), "z", axis=0, tiled=True)
    hidden = lax.all_gather(sel_hidden.reshape(rows, d), XC, axis=0, tiled=True)
    projected = jnp.dot(hidden, w, preferred_element_type=F32).astype(BF)
    merged = lax.all_to_all(projected.reshape(group, rows, cols), XC, 0, 0, tiled=True)

    frequency = 1.0 / BASE ** (jnp.arange(HD // 2, dtype=F32) * 2.0 / HD)
    index = jnp.arange(blocks, dtype=jnp.int32)
    local = (index[:, None] * block_len + sel_index[0]).reshape(rows)
    live = (jnp.arange(slots, dtype=jnp.int32)[None, :] < sel_count[0][:, None]).reshape(rows)
    cos, sin = half_turns((shard * tokens + local).astype(F32)[:, None] * frequency)
    lengths = lax.dynamic_index_in_dim(doc_lengths, y, 0, keepdims=False)
    nth = jnp.arange(lengths.shape[0], dtype=jnp.int32)
    ends = jnp.sum(jnp.where(nth[None, :] <= nth[:, None], lengths[None, :], 0), axis=1)
    here = shard * blocks + index
    first = jnp.sum(jnp.where(ends[None, :] <= here[:, None], lengths[None, :], 0), axis=1)
    kcos, ksin = half_turns((first * block_len).astype(F32)[:, None] * frequency)
    spots = jnp.where(live, local, -1).reshape(1, rows)

    wide = QH * HD + HD
    queries, fresh = call(
        rope_kernel,
        (jax.ShapeDtypeStruct((rows, wide), BF), jax.ShapeDtypeStruct((rows, kvw), BF)),
        [VM] * 4, (VM, VM),
        moved=4 * rows * (wide + kvw),
    )(merged, cos, sin, sel_index.reshape(rows, 1))

    def along(array, by):
        pairs = [(i, i + by) for i in range(n_seq) if 0 <= i + by < n_seq]
        return lax.ppermute(array, SEQ, pairs)

    q1, q2 = along(queries, -1), along(queries, -2)
    blended, num0, den0, p1, p2 = call(
        blend_kernel,
        (
            jax.ShapeDtypeStruct((tokens, kvw), BF),
            jax.ShapeDtypeStruct((rows, QH * HD), F32),
            jax.ShapeDtypeStruct((rows, HD), F32),
            jax.ShapeDtypeStruct((rows, wide), BF),
            jax.ShapeDtypeStruct((rows, wide), BF),
        ),
        [SM, SM] + [VM] * 7 + [ANY], (ANY, VM, VM, VM, VM),
        [
            pltpu.VMEM((tokens, kvw), BF),
            pltpu.VMEM((KH, 3 * GROUP * rows, HD), BF),
            pltpu.SemaphoreType.DMA((blocks,)),
            pltpu.SemaphoreType.DMA((blocks,)),
        ],
        flops=12 * rows * QH * HD * tokens,
        moved=8 * tokens * kvw,
    )(block_owner, me, spots, kcos, ksin, fresh, queries, q1, q2, incoming)
    r1, r2 = along(p1, 1), along(p2, 2)
    attended = call(
        merge_kernel,
        jax.ShapeDtypeStruct((rows, QH * HD), BF),
        [VM] * 5, VM,
        moved=12 * rows * QH * HD,
    )(num0, den0, r1, r2, live.astype(jnp.int32).reshape(rows, 1))
    return attended.reshape(1, blocks, slots, QH * HD), blended[None]


def solution(mesh):
    ny, n_seq = mesh.devices.shape
    fine = Mesh(
        mesh.devices.reshape(ny, n_seq // (NX * NC), NX, NC), ("y", "z", "x", "c")
    )
    return jax.shard_map(
        on_device,
        mesh=fine,
        in_specs=(
            P("y", SEQ, None, None),
            P(SEQ, "y"),
            P("y", SEQ, None),
            P(None, SEQ),
            P(),
            P("y", SEQ, None),
            P("y", SEQ),
        ),
        out_specs=(P("y", SEQ, None, None), P("y", SEQ, None)),
        check_vma=False,
    )
```

```python
import jax
import jax.numpy as jnp
from jax import lax
from jax.experimental import pallas as pl
from jax.experimental.pallas import tpu as pltpu
from jax.sharding import Mesh
from jax.sharding import PartitionSpec as P

QH = 16
KH = 4
HD = 128
GROUP = QH // KH
BLOCK = 128
BASE = 10000.0
NX, NC = 4, 2
CAP = 2
SEQ = ("z", "x", "c")
XC = ("x", "c")
F32 = jnp.float32
BF = jnp.bfloat16
VM = pl.BlockSpec(memory_space=pltpu.VMEM)
SM = pl.BlockSpec(memory_space=pltpu.SMEM)
ANY = pl.BlockSpec(memory_space=pl.ANY)


def call(kernel, out, ins, outs, scratch=(), flops=0, moved=0, vmem=8):
    return pl.pallas_call(
        kernel,
        out_shape=out,
        in_specs=ins,
        out_specs=outs,
        scratch_shapes=list(scratch),
        compiler_params=pltpu.CompilerParams(vmem_limit_bytes=vmem << 20),
        cost_estimate=pl.CostEstimate(flops=flops, bytes_accessed=moved, transcendentals=0),
    )


def pick_kernel(owner, me, pool, one_up, one_down, two_up, two_down, three_up, three_down, kept, sem):
    traces, blocks = owner.shape
    rows = pool.shape[0] // blocks
    mine = me[0]
    for slot in range(blocks):
        kept[slot] = 0
    slots = {
        1: (one_up.at[0], one_up.at[1]),
        2: (two_up.at[0], two_up.at[1]),
        3: (three_up.at[0], three_up.at[1]),
        4: (one_up.at[2], one_down.at[2]),
        5: (three_down.at[0], three_down.at[1]),
        6: (two_down.at[0], two_down.at[1]),
        7: (one_down.at[0], one_down.at[1]),
    }
    for d in range(traces):
        t = lax.rem(mine + d, traces)
        count = jnp.int32(0)
        for b in range(blocks):
            o = owner[t, b]
            slot = o % blocks
            hit = o // blocks == mine
            for nth in range(CAP if d else 0):

                @pl.when(hit & (count == nth))
                def _(slot=slot, out=slots[d][nth]):
                    start = pl.multiple_of(slot * rows, rows)
                    pltpu.make_async_copy(pool.at[pl.ds(start, rows)], out, sem.at[slot]).start()

            if d == 0:

                @pl.when(hit)
                def _(slot=slot):
                    kept[slot] = 1

            count = count + hit.astype(jnp.int32)
    for slot in range(blocks):

        @pl.when(kept[slot] == 0)
        def _(slot=slot):
            pltpu.make_async_copy(
                pool.at[pl.ds(slot * rows, rows)], two_up.at[0], sem.at[slot]
            ).wait()


def head(ref, n):
    per = ref.shape[2] // HD
    return ref[n // per, :, pl.ds((n % per) * HD, HD)]


def rotated(x, cos, sin):
    x = x.astype(F32)
    return x * cos + pltpu.roll(x, HD // 2, 1) * sin


def rope_kernel(proj, cos, sin, sel, q_out, fresh):
    for n in range(QH):
        q_out[:, n * HD : (n + 1) * HD] = rotated(head(proj, n), cos[...], sin[...]).astype(BF)
    rows = q_out.shape[0]
    q_out[:, QH * HD :] = jnp.broadcast_to(sel[...].astype(F32), (rows, HD)).astype(BF)
    for n in range(KH):
        k = rotated(head(proj, QH + n), cos[...], sin[...])
        fresh[:, n * HD : (n + 1) * HD] = k.astype(BF)
        fresh[:, (KH + n) * HD : (KH + n + 1) * HD] = head(proj, QH + KH + n)


def attend(queries, kv, stack, masks, put):
    n_q = queries[0].shape[0]
    tokens = kv.shape[0]
    size = GROUP * n_q
    lane = lax.broadcasted_iota(jnp.int32, (n_q, HD), 1)
    sums = [jnp.zeros((n_q, HD), F32) for _ in queries]
    for k in range(KH):
        keys = kv[:, k * HD : (k + 1) * HD]
        values = kv[:, (KH + k) * HD : (KH + k + 1) * HD]
        for i, q in enumerate(queries):
            for g in range(GROUP):
                h = k * GROUP + g
                stack[i, pl.ds(g * n_q, n_q), :] = q[:, h * HD : (h + 1) * HD]
            scores = lax.dot_general(
                stack[i], keys, (((1,), (1,)), ((), ())), preferred_element_type=F32
            )
            w = jnp.exp(scores * HD ** (-0.5))
            if masks[i] is not None:
                w = jnp.where(masks[i][None], w.reshape(GROUP, n_q, tokens), 0.0)
                w = w.reshape(size, tokens)
            total = jnp.sum(w, axis=1, keepdims=True)
            num = jnp.dot(w.astype(BF), values, preferred_element_type=F32)
            for g in range(GROUP):
                h = k * GROUP + g
                here = slice(g * n_q, (g + 1) * n_q)
                sums[i] = jnp.where(lane == h, total[here], sums[i])
                put(i, pl.ds(h * HD, HD), num[here])
    return sums


def token_of(q, tokens):
    n_q = q.shape[0]
    per = n_q // (tokens // BLOCK)
    block = lax.broadcasted_iota(jnp.int32, (n_q, 1), 0) // per
    return block * BLOCK + q[:, QH * HD : QH * HD + 1].astype(F32).astype(jnp.int32)


def blend_kernel(
    owner, me, kcos, ksin, spots, fresh, q0,
    pool, one_up, one_down, two_up, two_down, three_up, three_down,
    blended, kv, num0, den0, stack, sem, out_sem,
):
    traces, blocks = owner.shape
    rows = kv.shape[0] // blocks
    mine = me[0]
    own = [owner[mine, b] // blocks for b in range(blocks)]
    slots = {
        1: (one_up.at[0], one_up.at[1]),
        2: (two_up.at[0], two_up.at[1]),
        3: (three_up.at[0], three_up.at[1]),
        4: (three_up.at[2], three_down.at[2]),
        5: (three_down.at[0], three_down.at[1]),
        6: (two_down.at[0], two_down.at[1]),
        7: (one_down.at[0], one_down.at[1]),
    }
    for b in range(blocks):
        here = kv.at[pl.ds(b * rows, rows)]
        rank = jnp.int32(0)
        for e in range(b):
            rank = rank + (own[e] == own[b]).astype(jnp.int32)
        d = lax.rem(mine - own[b] + traces, traces)

        @pl.when(d == 0)
        def _(b=b, here=here):
            start = pl.multiple_of(owner[mine, b] % blocks * rows, rows)
            pltpu.make_async_copy(pool.at[pl.ds(start, rows)], here, sem.at[b]).start()

        for far in range(1, traces):
            for nth in range(CAP):

                @pl.when((d == far) & (rank == nth))
                def _(b=b, here=here, block=slots[far][nth]):
                    pltpu.make_async_copy(block, here, sem.at[b]).start()

    tokens, width = kv.shape
    n_q = q0.shape[0]
    ones = jnp.ones((n_q, HD), BF)
    for b in range(blocks):
        here = pl.ds(b * rows, rows)
        at = lax.broadcasted_iota(jnp.int32, (rows, n_q), 0) + b * rows
        hits = (at == spots[...]).astype(F32).astype(BF)
        chosen = jnp.dot(hits, ones, preferred_element_type=F32) > 0.5
        pltpu.make_async_copy(two_up.at[0], kv.at[here], sem.at[b]).wait()
        cos, sin = kcos[b : b + 1, :], ksin[b : b + 1, :]
        for n in range(width // HD):
            cols = pl.ds(n * HD, HD)
            x = kv[here, cols]
            x = rotated(x, cos, sin) if n < KH else x.astype(F32)
            placed = jnp.dot(hits, fresh[:, cols], preferred_element_type=F32)
            kv[here, cols] = jnp.where(chosen, placed, x).astype(BF)
        pltpu.make_async_copy(kv.at[here], blended.at[here], out_sem.at[b]).start()
    key = lax.broadcasted_iota(jnp.int32, (n_q, tokens), 1)

    def put(i, cols, num):
        num0[:, cols] = num

    (den0[...],) = attend([q0], kv, stack, [key <= token_of(q0, tokens)], put)
    for b in range(blocks):
        here = pl.ds(b * rows, rows)
        pltpu.make_async_copy(kv.at[here], blended.at[here], out_sem.at[b]).wait()


def remote_kernel(q1, q2, kv, p1, p2, stack):
    tokens = kv.shape[0]
    n_q = q1.shape[0]
    key = lax.broadcasted_iota(jnp.int32, (n_q, tokens), 1)

    def put(i, cols, num):
        (p1, p2)[i][:, cols] = num.astype(BF)

    sums = attend([q1, q2], kv, stack, [None, key > token_of(q2, tokens)], put)
    lane = lax.broadcasted_iota(jnp.int32, (n_q, HD), 1)
    for p, d in zip((p1, p2), sums):
        high = d.astype(BF)
        low = d - high.astype(F32)
        p[:, QH * HD :] = jnp.where(
            lane < QH, high.astype(F32), pltpu.roll(low, QH, 1)
        ).astype(BF)


def merge_kernel(num0, den0, r1, r2, live, out):
    total = den0[...]
    for r in (r1, r2):
        d = r[:, QH * HD :].astype(F32)
        total = total + d + pltpu.roll(d, HD - QH, 1)
    alive = live[...] > 0
    for h in range(QH):
        cols = pl.ds(h * HD, HD)
        num = num0[:, cols] + r1[:, cols].astype(F32) + r2[:, cols].astype(F32)
        out[:, cols] = jnp.where(alive, num / total[:, h : h + 1], 0.0).astype(BF)


def half_turns(angles):
    cos, sin = jnp.cos(angles), jnp.sin(angles)
    return jnp.concatenate([cos, cos], -1), jnp.concatenate([-sin, sin], -1)


def on_device(sel_hidden, w_qkv, cache_pool, block_owner, doc_lengths, sel_index, sel_count):
    ny, nz = lax.axis_size("y"), lax.axis_size("z")
    y = lax.axis_index("y")
    shard = lax.axis_index(SEQ)
    group = NX * NC
    n_seq = nz * group
    _, blocks, slots, d = sel_hidden.shape
    rows = blocks * slots
    tokens, kvw = cache_pool.shape[1:]
    block_len = tokens // blocks
    cols = w_qkv.shape[1]
    me = y.reshape(1).astype(jnp.int32)

    def turned(array, by):
        return lax.ppermute(array, "y", [(i, (i + by) % ny) for i in range(ny)])

    def room(n):
        return jax.ShapeDtypeStruct((n, block_len, kvw), BF)

    one_up, one_down, two_up, two_down, three_up, three_down = call(
        pick_kernel,
        (room(3), room(3), room(2), room(2), room(3), room(3)),
        [SM, SM, ANY], (ANY,) * 6,
        [pltpu.SMEM((blocks,), jnp.int32), pltpu.SemaphoreType.DMA((blocks,))],
        moved=4 * tokens * kvw,
    )(block_owner, me, cache_pool[0])
    one_up, w_qkv = lax.optimization_barrier((one_up, w_qkv))

    def crossed(m):
        pairs = [(a * group + b, (b ^ m) * group + a) for a in range(ny) for b in range(group)]
        return lax.ppermute(w_qkv, ("y", "x", "c"), pairs)

    def paired(mine, other, bit, axis):
        low = (y // bit) % 2 == 0
        return jnp.stack([jnp.where(low, mine, other), jnp.where(low, other, mine)], axis)

    w = paired(
        paired(crossed(0), crossed(4), 4, 0), paired(crossed(2), crossed(6), 4, 0), 2, 1
    )
    w = paired(w, lax.ppermute(w, "y", [(i, i ^ 1) for i in range(ny)]), 1, 2)
    w = w.reshape(-1, cols)
    w, one_up, one_down = lax.optimization_barrier((w, one_up, one_down))
    one_up, one_down = turned(one_up, 1), turned(one_down, -1)
    hidden = lax.all_gather(sel_hidden.reshape(rows, d), XC, axis=0, tiled=True)
    w, hidden, one_up, one_down = lax.optimization_barrier((w, hidden, one_up, one_down))
    w = lax.all_gather(w, "z", axis=0, tiled=True)
    two_up, two_down = turned(two_up, 2), turned(two_down, -2)
    three_up = turned(lax.dynamic_update_slice(three_up, one_up[2:], (2, 0, 0)), 3)
    three_down = turned(lax.dynamic_update_slice(three_down, one_down[2:], (2, 0, 0)), -3)
    projected = jnp.dot(hidden, w, preferred_element_type=F32).astype(BF)
    merged = lax.all_to_all(projected.reshape(group, rows, cols), XC, 0, 0, tiled=True)

    frequency = 1.0 / BASE ** (jnp.arange(HD // 2, dtype=F32) * 2.0 / HD)
    index = jnp.arange(blocks, dtype=jnp.int32)
    local = (index[:, None] * block_len + sel_index[0]).reshape(rows)
    live = (jnp.arange(slots, dtype=jnp.int32)[None, :] < sel_count[0][:, None]).reshape(rows)
    cos, sin = half_turns((shard * tokens + local).astype(F32)[:, None] * frequency)
    lengths = lax.dynamic_index_in_dim(doc_lengths, y, 0, keepdims=False)
    nth = jnp.arange(lengths.shape[0], dtype=jnp.int32)
    ends = jnp.sum(jnp.where(nth[None, :] <= nth[:, None], lengths[None, :], 0), axis=1)
    here = shard * blocks + index
    first = jnp.sum(jnp.where(ends[None, :] <= here[:, None], lengths[None, :], 0), axis=1)
    kcos, ksin = half_turns((first * block_len).astype(F32)[:, None] * frequency)
    spots = jnp.where(live, local, -1).reshape(1, rows)

    wide = QH * HD + HD
    queries, fresh = call(
        rope_kernel,
        (jax.ShapeDtypeStruct((rows, wide), BF), jax.ShapeDtypeStruct((rows, kvw), BF)),
        [VM] * 4, (VM, VM),
        moved=4 * rows * (wide + kvw),
    )(merged, cos, sin, sel_index.reshape(rows, 1))

    def along(array, by):
        pairs = [(i, i + by) for i in range(n_seq) if 0 <= i + by < n_seq]
        return lax.ppermute(array, SEQ, pairs)

    q1, q2 = along(queries, -1), along(queries, -2)
    blended, kv, num0, den0 = call(
        blend_kernel,
        (
            jax.ShapeDtypeStruct((tokens, kvw), BF),
            jax.ShapeDtypeStruct((tokens, kvw), BF),
            jax.ShapeDtypeStruct((rows, QH * HD), F32),
            jax.ShapeDtypeStruct((rows, HD), F32),
        ),
        [SM, SM] + [VM] * 5 + [ANY] * 7, (ANY, VM, VM, VM),
        [
            pltpu.VMEM((1, GROUP * rows, HD), BF),
            pltpu.SemaphoreType.DMA((blocks,)),
            pltpu.SemaphoreType.DMA((blocks,)),
        ],
        flops=4 * rows * QH * HD * tokens,
        moved=6 * tokens * kvw,
        vmem=20,
    )(
        block_owner, me, kcos, ksin, spots, fresh, queries, cache_pool[0],
        one_up, one_down, two_up, two_down, three_up, three_down,
    )
    p1, p2 = call(
        remote_kernel,
        (jax.ShapeDtypeStruct((rows, wide), BF),) * 2,
        [VM] * 3, (VM, VM),
        [pltpu.VMEM((2, GROUP * rows, HD), BF)],
        flops=8 * rows * QH * HD * tokens,
        moved=2 * tokens * kvw,
        vmem=20,
    )(q1, q2, kv)
    r1, r2 = along(p1, 1), along(p2, 2)
    attended = call(
        merge_kernel,
        jax.ShapeDtypeStruct((rows, QH * HD), BF),
        [VM] * 5, VM,
        moved=12 * rows * QH * HD,
    )(num0, den0, r1, r2, live.astype(jnp.int32).reshape(rows, 1))
    return attended.reshape(1, blocks, slots, QH * HD), blended[None]


def solution(mesh):
    ny, n_seq = mesh.devices.shape
    fine = Mesh(
        mesh.devices.reshape(ny, n_seq // (NX * NC), NX, NC), ("y", "z", "x", "c")
    )
    return jax.shard_map(
        on_device,
        mesh=fine,
        in_specs=(
            P("y", SEQ, None, None),
            P(SEQ, "y"),
            P("y", SEQ, None),
            P(None, SEQ),
            P(),
            P("y", SEQ, None),
            P("y", SEQ),
        ),
        out_specs=(P("y", SEQ, None, None), P("y", SEQ, None)),
        check_vma=False,
    )
```

```python
import jax
import jax.numpy as jnp
from jax import lax
from jax.experimental import pallas as pl
from jax.experimental.pallas import tpu as pltpu
from jax.sharding import Mesh
from jax.sharding import PartitionSpec as P

QH = 16
KH = 4
HD = 128
GROUP = QH // KH
BLOCK = 128
BASE = 10000.0
NX, NC = 4, 2
CAP = 2
SEQ = ("z", "x", "c")
XC = ("x", "c")
F32 = jnp.float32
BF = jnp.bfloat16
VM = pl.BlockSpec(memory_space=pltpu.VMEM)
SM = pl.BlockSpec(memory_space=pltpu.SMEM)
ANY = pl.BlockSpec(memory_space=pltpu.HBM)


def call(kernel, out, ins, outs, scratch=(), flops=0, moved=0, vmem=8):
    return pl.pallas_call(
        kernel,
        out_shape=out,
        in_specs=ins,
        out_specs=outs,
        scratch_shapes=list(scratch),
        compiler_params=pltpu.CompilerParams(vmem_limit_bytes=vmem << 20),
        cost_estimate=pl.CostEstimate(flops=flops, bytes_accessed=moved, transcendentals=0),
    )


def kept(*arrays):
    return [pltpu.with_memory_space_constraint(a, pltpu.HBM) for a in arrays]


def pick_kernel(owner, me, pool, one_up, one_down, two_up, two_down, three_up, three_down, stays, sem):
    traces, blocks = owner.shape
    rows = pool.shape[0] // blocks
    mine = me[0]
    for slot in range(blocks):
        stays[slot] = 0
    slots = {
        1: (one_up.at[0], one_up.at[1]),
        2: (two_up.at[0], two_up.at[1]),
        3: (three_up.at[0], three_up.at[1]),
        4: (one_up.at[2], one_down.at[2]),
        5: (three_down.at[0], three_down.at[1]),
        6: (two_down.at[0], two_down.at[1]),
        7: (one_down.at[0], one_down.at[1]),
    }
    for d in range(traces):
        t = lax.rem(mine + d, traces)
        count = jnp.int32(0)
        for b in range(blocks):
            o = owner[t, b]
            slot = o % blocks
            hit = o // blocks == mine
            for nth in range(CAP if d else 0):

                @pl.when(hit & (count == nth))
                def _(slot=slot, out=slots[d][nth]):
                    start = pl.multiple_of(slot * rows, rows)
                    pltpu.make_async_copy(pool.at[pl.ds(start, rows)], out, sem.at[slot]).start()

            if d == 0:

                @pl.when(hit)
                def _(slot=slot):
                    stays[slot] = 1

            count = count + hit.astype(jnp.int32)
    for slot in range(blocks):

        @pl.when(stays[slot] == 0)
        def _(slot=slot):
            pltpu.make_async_copy(
                pool.at[pl.ds(slot * rows, rows)], two_up.at[0], sem.at[slot]
            ).wait()


def project_kernel(hidden, w, out, total):
    step = pl.program_id(0)
    product = jnp.dot(hidden[...], w[...], preferred_element_type=F32)

    @pl.when(step == 0)
    def _():
        total[...] = product

    @pl.when(step > 0)
    def _():
        total[...] += product

    @pl.when(step == pl.num_programs(0) - 1)
    def _():
        out[...] = total[...].astype(BF).reshape(out.shape)


def head(ref, n):
    per = ref.shape[2] // HD
    return ref[n // per, :, pl.ds((n % per) * HD, HD)]


def rotated(x, cos, sin):
    x = x.astype(F32)
    return x * cos + pltpu.roll(x, HD // 2, 1) * sin


def rope_kernel(proj, cos, sin, sel, q_out, fresh):
    for n in range(QH):
        q_out[:, n * HD : (n + 1) * HD] = rotated(head(proj, n), cos[...], sin[...]).astype(BF)
    rows = q_out.shape[0]
    q_out[:, QH * HD :] = jnp.broadcast_to(sel[...].astype(F32), (rows, HD)).astype(BF)
    for n in range(KH):
        k = rotated(head(proj, QH + n), cos[...], sin[...])
        fresh[:, n * HD : (n + 1) * HD] = k.astype(BF)
        fresh[:, (KH + n) * HD : (KH + n + 1) * HD] = head(proj, QH + KH + n)


def attend(queries, kv, stack, masks, put):
    n_q = queries[0].shape[0]
    tokens = kv.shape[0]
    size = GROUP * n_q
    lane = lax.broadcasted_iota(jnp.int32, (n_q, HD), 1)
    sums = [jnp.zeros((n_q, HD), F32) for _ in queries]
    for k in range(KH):
        keys = kv[:, k * HD : (k + 1) * HD]
        values = kv[:, (KH + k) * HD : (KH + k + 1) * HD]
        for i, q in enumerate(queries):
            for g in range(GROUP):
                h = k * GROUP + g
                stack[i, pl.ds(g * n_q, n_q), :] = q[:, h * HD : (h + 1) * HD]
            scores = lax.dot_general(
                stack[i], keys, (((1,), (1,)), ((), ())), preferred_element_type=F32
            )
            w = jnp.exp(scores * HD ** (-0.5))
            if masks[i] is not None:
                w = jnp.where(masks[i][None], w.reshape(GROUP, n_q, tokens), 0.0)
                w = w.reshape(size, tokens)
            total = jnp.sum(w, axis=1, keepdims=True)
            num = jnp.dot(w.astype(BF), values, preferred_element_type=F32)
            for g in range(GROUP):
                h = k * GROUP + g
                here = slice(g * n_q, (g + 1) * n_q)
                sums[i] = jnp.where(lane == h, total[here], sums[i])
                put(i, pl.ds(h * HD, HD), num[here])
    return sums


def token_of(q, tokens):
    n_q = q.shape[0]
    per = n_q // (tokens // BLOCK)
    block = lax.broadcasted_iota(jnp.int32, (n_q, 1), 0) // per
    return block * BLOCK + q[:, QH * HD : QH * HD + 1].astype(F32).astype(jnp.int32)


def blend_kernel(
    owner, me, kcos, ksin, spots, fresh,
    pool, one_up, one_down, two_up, two_down, three_up, three_down,
    blended, kv, sem, out_sem,
):
    traces, blocks = owner.shape
    rows = kv.shape[0] // blocks
    mine = me[0]
    own = [owner[mine, b] // blocks for b in range(blocks)]
    slots = {
        1: (one_up.at[0], one_up.at[1]),
        2: (two_up.at[0], two_up.at[1]),
        3: (three_up.at[0], three_up.at[1]),
        4: (three_up.at[2], three_down.at[2]),
        5: (three_down.at[0], three_down.at[1]),
        6: (two_down.at[0], two_down.at[1]),
        7: (one_down.at[0], one_down.at[1]),
    }
    for b in range(blocks):
        here = kv.at[pl.ds(b * rows, rows)]
        rank = jnp.int32(0)
        for e in range(b):
            rank = rank + (own[e] == own[b]).astype(jnp.int32)
        d = lax.rem(mine - own[b] + traces, traces)

        @pl.when(d == 0)
        def _(b=b, here=here):
            start = pl.multiple_of(owner[mine, b] % blocks * rows, rows)
            pltpu.make_async_copy(pool.at[pl.ds(start, rows)], here, sem.at[b]).start()

        for far in range(1, traces):
            for nth in range(CAP):

                @pl.when((d == far) & (rank == nth))
                def _(b=b, here=here, block=slots[far][nth]):
                    pltpu.make_async_copy(block, here, sem.at[b]).start()

    width = kv.shape[1]
    n_q = fresh.shape[0]
    ones = jnp.ones((n_q, HD), BF)
    for b in range(blocks):
        here = pl.ds(b * rows, rows)
        at = lax.broadcasted_iota(jnp.int32, (rows, n_q), 0) + b * rows
        hits = (at == spots[...]).astype(F32).astype(BF)
        chosen = jnp.dot(hits, ones, preferred_element_type=F32) > 0.5
        pltpu.make_async_copy(two_up.at[0], kv.at[here], sem.at[b]).wait()
        cos, sin = kcos[b : b + 1, :], ksin[b : b + 1, :]
        for n in range(width // HD):
            cols = pl.ds(n * HD, HD)
            x = kv[here, cols]
            x = rotated(x, cos, sin) if n < KH else x.astype(F32)
            placed = jnp.dot(hits, fresh[:, cols], preferred_element_type=F32)
            kv[here, cols] = jnp.where(chosen, placed, x).astype(BF)
        pltpu.make_async_copy(kv.at[here], blended.at[here], out_sem.at[b]).start()
    for b in range(blocks):
        here = pl.ds(b * rows, rows)
        pltpu.make_async_copy(kv.at[here], blended.at[here], out_sem.at[b]).wait()


def own_kernel(q0, kv, num0, den0, stack):
    tokens = kv.shape[0]
    n_q = q0.shape[0]
    key = lax.broadcasted_iota(jnp.int32, (n_q, tokens), 1)

    def put(i, cols, num):
        num0[:, cols] = num

    (den0[...],) = attend([q0], kv, stack, [key <= token_of(q0, tokens)], put)


def remote_kernel(q1, q2, kv, p1, p2, stack):
    tokens = kv.shape[0]
    n_q = q1.shape[0]
    key = lax.broadcasted_iota(jnp.int32, (n_q, tokens), 1)

    def put(i, cols, num):
        (p1, p2)[i][:, cols] = num.astype(BF)

    sums = attend([q1, q2], kv, stack, [None, key > token_of(q2, tokens)], put)
    lane = lax.broadcasted_iota(jnp.int32, (n_q, HD), 1)
    for p, d in zip((p1, p2), sums):
        high = d.astype(BF)
        low = d - high.astype(F32)
        p[:, QH * HD :] = jnp.where(
            lane < QH, high.astype(F32), pltpu.roll(low, QH, 1)
        ).astype(BF)


def merge_kernel(num0, den0, r1, r2, live, out):
    total = den0[...]
    for r in (r1, r2):
        d = r[:, QH * HD :].astype(F32)
        total = total + d + pltpu.roll(d, HD - QH, 1)
    alive = live[...] > 0
    for h in range(QH):
        cols = pl.ds(h * HD, HD)
        num = num0[:, cols] + r1[:, cols].astype(F32) + r2[:, cols].astype(F32)
        out[:, cols] = jnp.where(alive, num / total[:, h : h + 1], 0.0).astype(BF)


def half_turns(angles):
    cos, sin = jnp.cos(angles), jnp.sin(angles)
    return jnp.concatenate([cos, cos], -1), jnp.concatenate([-sin, sin], -1)


def on_device(sel_hidden, w_qkv, cache_pool, block_owner, doc_lengths, sel_index, sel_count):
    ny, nz = lax.axis_size("y"), lax.axis_size("z")
    y = lax.axis_index("y")
    shard = lax.axis_index(SEQ)
    group = NX * NC
    n_seq = nz * group
    _, blocks, slots, d = sel_hidden.shape
    rows = blocks * slots
    tokens, kvw = cache_pool.shape[1:]
    block_len = tokens // blocks
    cols = w_qkv.shape[1]
    me = y.reshape(1).astype(jnp.int32)

    def around(array, axis, by):
        n = lax.axis_size(axis)
        return lax.ppermute(array, axis, [(i, (i + by) % n) for i in range(n)])

    def turned(array, by):
        return around(array, "y", by)

    def room(n):
        return pltpu.HBM((n, block_len, kvw), BF)

    one_up, one_down, two_up, two_down, three_up, three_down = call(
        pick_kernel,
        (room(3), room(3), room(2), room(2), room(3), room(3)),
        [SM, SM, ANY], (ANY,) * 6,
        [pltpu.SMEM((blocks,), jnp.int32), pltpu.SemaphoreType.DMA((blocks,))],
        moved=4 * tokens * kvw,
    )(block_owner, me, *kept(cache_pool[0]))
    one_up, w_qkv = lax.optimization_barrier((one_up, w_qkv))

    pairs = [(a * group + b, b * group + a) for a in range(ny) for b in range(group)]
    w = lax.ppermute(w_qkv, ("y", "x", "c"), pairs)
    w = jnp.broadcast_to(w[None], (ny,) + w_qkv.shape)
    w = lax.all_to_all(w, "y", 0, 0, tiled=True).reshape(-1, cols)
    w, one_up, one_down = lax.optimization_barrier((w, one_up, one_down))
    one_up, one_down = turned(one_up, 1), turned(one_down, -1)
    hidden = lax.all_gather(sel_hidden.reshape(rows, d), XC, axis=0, tiled=True)
    w, hidden, one_up, one_down = lax.optimization_barrier((w, hidden, one_up, one_down))
    w = lax.all_gather(w, "z", axis=0, tiled=True)
    two_up, two_down = turned(two_up, 2), turned(two_down, -2)
    three_up = turned(lax.dynamic_update_slice(three_up, one_up[2:], (2, 0, 0)), 3)
    three_down = turned(lax.dynamic_update_slice(three_down, one_down[2:], (2, 0, 0)), -3)
    depth = 512
    projected = pl.pallas_call(
        project_kernel,
        out_shape=jax.ShapeDtypeStruct((group, rows, cols), BF),
        grid=(d // depth,),
        in_specs=[
            pl.BlockSpec((group * rows, depth), lambda i: (0, i)),
            pl.BlockSpec((depth, cols), lambda i: (i, 0)),
        ],
        out_specs=pl.BlockSpec((group, rows, cols), lambda i: (0, 0, 0)),
        scratch_shapes=[pltpu.VMEM((group * rows, cols), F32)],
        compiler_params=pltpu.CompilerParams(vmem_limit_bytes=12 << 20),
        cost_estimate=pl.CostEstimate(
            flops=2 * group * rows * cols * d,
            bytes_accessed=2 * d * (group * rows + cols),
            transcendentals=0,
        ),
    )(*kept(hidden, w))
    merged = lax.all_to_all(projected, XC, 0, 0, tiled=True)

    frequency = 1.0 / BASE ** (jnp.arange(HD // 2, dtype=F32) * 2.0 / HD)
    index = jnp.arange(blocks, dtype=jnp.int32)
    local = (index[:, None] * block_len + sel_index[0]).reshape(rows)
    live = (jnp.arange(slots, dtype=jnp.int32)[None, :] < sel_count[0][:, None]).reshape(rows)
    cos, sin = half_turns((shard * tokens + local).astype(F32)[:, None] * frequency)
    lengths = lax.dynamic_index_in_dim(doc_lengths, y, 0, keepdims=False)
    nth = jnp.arange(lengths.shape[0], dtype=jnp.int32)
    ends = jnp.sum(jnp.where(nth[None, :] <= nth[:, None], lengths[None, :], 0), axis=1)
    here = shard * blocks + index
    first = jnp.sum(jnp.where(ends[None, :] <= here[:, None], lengths[None, :], 0), axis=1)
    kcos, ksin = half_turns((first * block_len).astype(F32)[:, None] * frequency)
    spots = jnp.where(live, local, -1).reshape(1, rows)

    wide = QH * HD + HD
    queries, fresh = call(
        rope_kernel,
        (jax.ShapeDtypeStruct((rows, wide), BF), jax.ShapeDtypeStruct((rows, kvw), BF)),
        [VM] * 4, (VM, VM),
        moved=4 * rows * (wide + kvw),
    )(merged, cos, sin, sel_index.reshape(rows, 1))

    def along(array, by):
        pairs = [(i, i + by) for i in range(n_seq) if 0 <= i + by < n_seq]
        return lax.ppermute(array, SEQ, pairs)

    q1, q2 = along(queries, -1), along(queries, -2)
    blended, kv = call(
        blend_kernel,
        (jax.ShapeDtypeStruct((tokens, kvw), BF),) * 2,
        [SM, SM] + [VM] * 4 + [ANY] * 7, (ANY, VM),
        [pltpu.SemaphoreType.DMA((blocks,)), pltpu.SemaphoreType.DMA((blocks,))],
        moved=6 * tokens * kvw,
    )(
        block_owner, me, kcos, ksin, spots, fresh,
        *kept(cache_pool[0], one_up, one_down, two_up, two_down, three_up, three_down),
    )
    p1, p2 = call(
        remote_kernel,
        (jax.ShapeDtypeStruct((rows, wide), BF),) * 2,
        [VM] * 3, (VM, VM),
        [pltpu.VMEM((2, GROUP * rows, HD), BF)],
        flops=8 * rows * QH * HD * tokens,
        moved=2 * tokens * kvw,
        vmem=20,
    )(q1, q2, kv)
    whole, p1, p2 = lax.optimization_barrier((blended, p1, p2))
    r1, r2 = along(p1, 1), along(p2, 2)
    num0, den0 = call(
        own_kernel,
        (jax.ShapeDtypeStruct((rows, QH * HD), F32), jax.ShapeDtypeStruct((rows, HD), F32)),
        [VM] * 2, (VM, VM),
        [pltpu.VMEM((1, GROUP * rows, HD), BF)],
        flops=4 * rows * QH * HD * tokens,
        moved=2 * tokens * kvw,
        vmem=20,
    )(queries, whole)
    attended = call(
        merge_kernel,
        jax.ShapeDtypeStruct((rows, QH * HD), BF),
        [VM] * 5, VM,
        moved=12 * rows * QH * HD,
    )(num0, den0, r1, r2, live.astype(jnp.int32).reshape(rows, 1))
    return attended.reshape(1, blocks, slots, QH * HD), blended[None]


def solution(mesh):
    ny, n_seq = mesh.devices.shape
    fine = Mesh(
        mesh.devices.reshape(ny, n_seq // (NX * NC), NX, NC), ("y", "z", "x", "c")
    )
    return jax.shard_map(
        on_device,
        mesh=fine,
        in_specs=(
            P("y", SEQ, None, None),
            P(SEQ, "y"),
            P("y", SEQ, None),
            P(None, SEQ),
            P(),
            P("y", SEQ, None),
            P("y", SEQ),
        ),
        out_specs=(P("y", SEQ, None, None), P("y", SEQ, None)),
        check_vma=False,
    )
```

```python
import jax
import jax.numpy as jnp
from jax import lax
from jax.experimental import pallas as pl
from jax.experimental.pallas import tpu as pltpu
from jax.sharding import Mesh
from jax.sharding import PartitionSpec as P

QH = 16
KH = 4
HD = 128
GROUP = QH // KH
BLOCK = 128
BASE = 10000.0
NX, NC = 4, 2
CAP = 2
SEQ = ("z", "x", "c")
XC = ("x", "c")
F32 = jnp.float32
BF = jnp.bfloat16
VM = pl.BlockSpec(memory_space=pltpu.VMEM)
SM = pl.BlockSpec(memory_space=pltpu.SMEM)
ANY = pl.BlockSpec(memory_space=pltpu.HBM)


def call(kernel, out, ins, outs, scratch=(), flops=0, moved=0, vmem=8):
    return pl.pallas_call(
        kernel,
        out_shape=out,
        in_specs=ins,
        out_specs=outs,
        scratch_shapes=list(scratch),
        compiler_params=pltpu.CompilerParams(vmem_limit_bytes=vmem << 20),
        cost_estimate=pl.CostEstimate(flops=flops, bytes_accessed=moved, transcendentals=0),
    )


def kept(*arrays):
    return [pltpu.with_memory_space_constraint(a, pltpu.HBM) for a in arrays]


def pick_kernel(owner, me, pool, one_up, one_down, two_up, two_down, three_up, three_down, stays, staged, sem, out_sem):
    traces, blocks = owner.shape
    rows = pool.shape[0] // blocks
    mine = me[0]
    for slot in range(blocks):
        stays[slot] = 0
        here = pl.ds(slot * rows, rows)
        pltpu.make_async_copy(pool.at[here], staged.at[here], sem.at[slot]).start()
    for slot in range(blocks):
        here = pl.ds(slot * rows, rows)
        pltpu.make_async_copy(pool.at[here], staged.at[here], sem.at[slot]).wait()
    slots = {
        1: (one_up.at[0], one_up.at[1]),
        2: (two_up.at[0], two_up.at[1]),
        3: (three_up.at[0], three_up.at[1]),
        4: (one_up.at[2], one_down.at[2]),
        5: (three_down.at[0], three_down.at[1]),
        6: (two_down.at[0], two_down.at[1]),
        7: (one_down.at[0], one_down.at[1]),
    }
    for d in range(traces):
        t = lax.rem(mine + d, traces)
        count = jnp.int32(0)
        for b in range(blocks):
            o = owner[t, b]
            slot = o % blocks
            hit = o // blocks == mine
            for nth in range(CAP if d else 0):

                @pl.when(hit & (count == nth))
                def _(slot=slot, out=slots[d][nth]):
                    start = pl.multiple_of(slot * rows, rows)
                    pltpu.make_async_copy(
                        staged.at[pl.ds(start, rows)], out, out_sem.at[slot]
                    ).start()

            if d == 0:

                @pl.when(hit)
                def _(slot=slot):
                    stays[slot] = 1

            count = count + hit.astype(jnp.int32)
    for slot in range(blocks):

        @pl.when(stays[slot] == 0)
        def _(slot=slot):
            pltpu.make_async_copy(
                staged.at[pl.ds(slot * rows, rows)], two_up.at[0], out_sem.at[slot]
            ).wait()


def head(ref, n):
    per = ref.shape[2] // HD
    return ref[n // per, :, pl.ds((n % per) * HD, HD)]


def rotated(x, cos, sin):
    x = x.astype(F32)
    return x * cos + pltpu.roll(x, HD // 2, 1) * sin


def rope_kernel(proj, cos, sin, sel, q_out, fresh):
    for n in range(QH):
        q_out[:, n * HD : (n + 1) * HD] = rotated(head(proj, n), cos[...], sin[...]).astype(BF)
    rows = q_out.shape[0]
    q_out[:, QH * HD :] = jnp.broadcast_to(sel[...].astype(F32), (rows, HD)).astype(BF)
    for n in range(KH):
        k = rotated(head(proj, QH + n), cos[...], sin[...])
        fresh[:, n * HD : (n + 1) * HD] = k.astype(BF)
        fresh[:, (KH + n) * HD : (KH + n + 1) * HD] = head(proj, QH + KH + n)


def attend(queries, kv, stack, masks, put):
    n_q = queries[0].shape[0]
    tokens = kv.shape[0]
    size = GROUP * n_q
    lane = lax.broadcasted_iota(jnp.int32, (n_q, HD), 1)
    sums = [jnp.zeros((n_q, HD), F32) for _ in queries]
    for k in range(KH):
        keys = kv[:, k * HD : (k + 1) * HD]
        values = kv[:, (KH + k) * HD : (KH + k + 1) * HD]
        for i, q in enumerate(queries):
            for g in range(GROUP):
                h = k * GROUP + g
                stack[i, pl.ds(g * n_q, n_q), :] = q[:, h * HD : (h + 1) * HD]
            scores = lax.dot_general(
                stack[i], keys, (((1,), (1,)), ((), ())), preferred_element_type=F32
            )
            w = jnp.exp(scores * HD ** (-0.5))
            if masks[i] is not None:
                w = jnp.where(masks[i][None], w.reshape(GROUP, n_q, tokens), 0.0)
                w = w.reshape(size, tokens)
            total = jnp.sum(w, axis=1, keepdims=True)
            num = jnp.dot(w.astype(BF), values, preferred_element_type=F32)
            for g in range(GROUP):
                h = k * GROUP + g
                here = slice(g * n_q, (g + 1) * n_q)
                sums[i] = jnp.where(lane == h, total[here], sums[i])
                put(i, pl.ds(h * HD, HD), num[here])
    return sums


def token_of(q, tokens):
    n_q = q.shape[0]
    per = n_q // (tokens // BLOCK)
    block = lax.broadcasted_iota(jnp.int32, (n_q, 1), 0) // per
    return block * BLOCK + q[:, QH * HD : QH * HD + 1].astype(F32).astype(jnp.int32)


def blend_kernel(
    owner, me, kcos, ksin, spots, fresh,
    pool, one_up, one_down, two_up, two_down, three_up, three_down,
    blended, kv, sem, out_sem,
):
    traces, blocks = owner.shape
    rows = kv.shape[0] // blocks
    mine = me[0]
    own = [owner[mine, b] // blocks for b in range(blocks)]
    slots = {
        1: (one_up.at[0], one_up.at[1]),
        2: (two_up.at[0], two_up.at[1]),
        3: (three_up.at[0], three_up.at[1]),
        4: (three_up.at[2], three_down.at[2]),
        5: (three_down.at[0], three_down.at[1]),
        6: (two_down.at[0], two_down.at[1]),
        7: (one_down.at[0], one_down.at[1]),
    }
    for b in range(blocks):
        here = kv.at[pl.ds(b * rows, rows)]
        rank = jnp.int32(0)
        for e in range(b):
            rank = rank + (own[e] == own[b]).astype(jnp.int32)
        d = lax.rem(mine - own[b] + traces, traces)

        @pl.when(d == 0)
        def _(b=b, here=here):
            start = pl.multiple_of(owner[mine, b] % blocks * rows, rows)
            pltpu.make_async_copy(pool.at[pl.ds(start, rows)], here, sem.at[b]).start()

        for far in range(1, traces):
            for nth in range(CAP):

                @pl.when((d == far) & (rank == nth))
                def _(b=b, here=here, block=slots[far][nth]):
                    pltpu.make_async_copy(block, here, sem.at[b]).start()

    width = kv.shape[1]
    n_q = fresh.shape[0]
    ones = jnp.ones((n_q, HD), BF)
    for b in range(blocks):
        here = pl.ds(b * rows, rows)
        at = lax.broadcasted_iota(jnp.int32, (rows, n_q), 0) + b * rows
        hits = (at == spots[...]).astype(F32).astype(BF)
        chosen = jnp.dot(hits, ones, preferred_element_type=F32) > 0.5
        pltpu.make_async_copy(two_up.at[0], kv.at[here], sem.at[b]).wait()
        cos, sin = kcos[b : b + 1, :], ksin[b : b + 1, :]
        for n in range(width // HD):
            cols = pl.ds(n * HD, HD)
            x = kv[here, cols]
            x = rotated(x, cos, sin) if n < KH else x.astype(F32)
            placed = jnp.dot(hits, fresh[:, cols], preferred_element_type=F32)
            kv[here, cols] = jnp.where(chosen, placed, x).astype(BF)
        pltpu.make_async_copy(kv.at[here], blended.at[here], out_sem.at[b]).start()
    for b in range(blocks):
        here = pl.ds(b * rows, rows)
        pltpu.make_async_copy(kv.at[here], blended.at[here], out_sem.at[b]).wait()


def own_kernel(q0, kv, num0, den0, stack):
    tokens = kv.shape[0]
    n_q = q0.shape[0]
    key = lax.broadcasted_iota(jnp.int32, (n_q, tokens), 1)

    def put(i, cols, num):
        num0[:, cols] = num

    (den0[...],) = attend([q0], kv, stack, [key <= token_of(q0, tokens)], put)


def remote_kernel(q1, q2, kv, p1, p2, stack):
    tokens = kv.shape[0]
    n_q = q1.shape[0]
    key = lax.broadcasted_iota(jnp.int32, (n_q, tokens), 1)

    def put(i, cols, num):
        (p1, p2)[i][:, cols] = num.astype(BF)

    sums = attend([q1, q2], kv, stack, [None, key > token_of(q2, tokens)], put)
    lane = lax.broadcasted_iota(jnp.int32, (n_q, HD), 1)
    for p, d in zip((p1, p2), sums):
        high = d.astype(BF)
        low = d - high.astype(F32)
        p[:, QH * HD :] = jnp.where(
            lane < QH, high.astype(F32), pltpu.roll(low, QH, 1)
        ).astype(BF)


def merge_kernel(num0, den0, r1, r2, live, out):
    total = den0[...]
    for r in (r1, r2):
        d = r[:, QH * HD :].astype(F32)
        total = total + d + pltpu.roll(d, HD - QH, 1)
    alive = live[...] > 0
    for h in range(QH):
        cols = pl.ds(h * HD, HD)
        num = num0[:, cols] + r1[:, cols].astype(F32) + r2[:, cols].astype(F32)
        out[:, cols] = jnp.where(alive, num / total[:, h : h + 1], 0.0).astype(BF)


def half_turns(angles):
    cos, sin = jnp.cos(angles), jnp.sin(angles)
    return jnp.concatenate([cos, cos], -1), jnp.concatenate([-sin, sin], -1)


def on_device(sel_hidden, w_qkv, cache_pool, block_owner, doc_lengths, sel_index, sel_count):
    ny, nz = lax.axis_size("y"), lax.axis_size("z")
    y = lax.axis_index("y")
    shard = lax.axis_index(SEQ)
    group = NX * NC
    n_seq = nz * group
    _, blocks, slots, d = sel_hidden.shape
    rows = blocks * slots
    tokens, kvw = cache_pool.shape[1:]
    block_len = tokens // blocks
    cols = w_qkv.shape[1]
    me = y.reshape(1).astype(jnp.int32)

    def turned(array, by):
        return lax.ppermute(array, "y", [(i, (i + by) % ny) for i in range(ny)])

    def room(n):
        return pltpu.HBM((n, block_len, kvw), BF)

    one_up, one_down, two_up, two_down, three_up, three_down = call(
        pick_kernel,
        (room(3), room(3), room(2), room(2), room(3), room(3)),
        [SM, SM, ANY], (ANY,) * 6,
        [
            pltpu.SMEM((blocks,), jnp.int32),
            pltpu.VMEM((tokens, kvw), BF),
            pltpu.SemaphoreType.DMA((blocks,)),
            pltpu.SemaphoreType.DMA((blocks,)),
        ],
        moved=4 * tokens * kvw,
    )(block_owner, me, *kept(cache_pool[0]))
    one_up, w_qkv = lax.optimization_barrier((one_up, w_qkv))
    one_up, one_down = turned(one_up, 1), turned(one_down, -1)

    def crossed(m):
        pairs = [(a * group + b, (b ^ m) * group + a) for a in range(ny) for b in range(group)]
        return lax.ppermute(w_qkv, ("y", "x", "c"), pairs)

    def paired(mine, other, bit, axis):
        low = (y // bit) % 2 == 0
        return jnp.stack([jnp.where(low, mine, other), jnp.where(low, other, mine)], axis)

    w = paired(
        paired(crossed(0), crossed(4), 4, 0), paired(crossed(2), crossed(6), 4, 0), 2, 1
    )
    w, one_up, one_down = lax.optimization_barrier((w, one_up, one_down))
    w = paired(w, lax.ppermute(w, "y", [(i, i ^ 1) for i in range(ny)]), 1, 2).reshape(-1, cols)
    w, two_up, two_down, one_up, one_down = lax.optimization_barrier(
        (w, two_up, two_down, one_up, one_down)
    )
    hidden = lax.all_gather(sel_hidden.reshape(rows, d), XC, axis=0, tiled=True)
    w, hidden = lax.optimization_barrier((w, hidden))
    w = lax.all_gather(w, "z", axis=0, tiled=True)
    two_up, two_down = turned(two_up, 2), turned(two_down, -2)
    two_up, two_down, three_up, three_down = lax.optimization_barrier(
        (two_up, two_down, three_up, three_down)
    )
    three_up = turned(lax.dynamic_update_slice(three_up, one_up[2:], (2, 0, 0)), 3)
    three_down = turned(lax.dynamic_update_slice(three_down, one_down[2:], (2, 0, 0)), -3)
    projected = jnp.dot(hidden, w, preferred_element_type=F32).astype(BF)
    projected = projected.reshape(group, rows, cols)
    merged = lax.all_to_all(projected, XC, 0, 0, tiled=True)

    frequency = 1.0 / BASE ** (jnp.arange(HD // 2, dtype=F32) * 2.0 / HD)
    index = jnp.arange(blocks, dtype=jnp.int32)
    local = (index[:, None] * block_len + sel_index[0]).reshape(rows)
    live = (jnp.arange(slots, dtype=jnp.int32)[None, :] < sel_count[0][:, None]).reshape(rows)
    cos, sin = half_turns((shard * tokens + local).astype(F32)[:, None] * frequency)
    lengths = lax.dynamic_index_in_dim(doc_lengths, y, 0, keepdims=False)
    nth = jnp.arange(lengths.shape[0], dtype=jnp.int32)
    ends = jnp.sum(jnp.where(nth[None, :] <= nth[:, None], lengths[None, :], 0), axis=1)
    here = shard * blocks + index
    first = jnp.sum(jnp.where(ends[None, :] <= here[:, None], lengths[None, :], 0), axis=1)
    kcos, ksin = half_turns((first * block_len).astype(F32)[:, None] * frequency)
    spots = jnp.where(live, local, -1).reshape(1, rows)

    wide = QH * HD + HD
    queries, fresh = call(
        rope_kernel,
        (jax.ShapeDtypeStruct((rows, wide), BF), jax.ShapeDtypeStruct((rows, kvw), BF)),
        [VM] * 4, (VM, VM),
        moved=4 * rows * (wide + kvw),
    )(merged, cos, sin, sel_index.reshape(rows, 1))

    def along(array, by):
        pairs = [(i, i + by) for i in range(n_seq) if 0 <= i + by < n_seq]
        return lax.ppermute(array, SEQ, pairs)

    q1, q2 = along(queries, -1), along(queries, -2)
    blended, kv = call(
        blend_kernel,
        (jax.ShapeDtypeStruct((tokens, kvw), BF),) * 2,
        [SM, SM] + [VM] * 4 + [ANY] * 7, (ANY, VM),
        [pltpu.SemaphoreType.DMA((blocks,)), pltpu.SemaphoreType.DMA((blocks,))],
        moved=6 * tokens * kvw,
    )(
        block_owner, me, kcos, ksin, spots, fresh,
        *kept(cache_pool[0], one_up, one_down, two_up, two_down, three_up, three_down),
    )
    p1, p2 = call(
        remote_kernel,
        (jax.ShapeDtypeStruct((rows, wide), BF),) * 2,
        [VM] * 3, (VM, VM),
        [pltpu.VMEM((2, GROUP * rows, HD), BF)],
        flops=8 * rows * QH * HD * tokens,
        moved=2 * tokens * kvw,
        vmem=20,
    )(q1, q2, kv)
    whole, p1, p2 = lax.optimization_barrier((blended, p1, p2))
    r1, r2 = along(p1, 1), along(p2, 2)
    num0, den0 = call(
        own_kernel,
        (jax.ShapeDtypeStruct((rows, QH * HD), F32), jax.ShapeDtypeStruct((rows, HD), F32)),
        [VM] * 2, (VM, VM),
        [pltpu.VMEM((1, GROUP * rows, HD), BF)],
        flops=4 * rows * QH * HD * tokens,
        moved=2 * tokens * kvw,
        vmem=20,
    )(queries, whole)
    attended = call(
        merge_kernel,
        jax.ShapeDtypeStruct((rows, QH * HD), BF),
        [VM] * 5, VM,
        moved=12 * rows * QH * HD,
    )(num0, den0, r1, r2, live.astype(jnp.int32).reshape(rows, 1))
    return attended.reshape(1, blocks, slots, QH * HD), blended[None]


def solution(mesh):
    ny, n_seq = mesh.devices.shape
    fine = Mesh(
        mesh.devices.reshape(ny, n_seq // (NX * NC), NX, NC), ("y", "z", "x", "c")
    )
    return jax.shard_map(
        on_device,
        mesh=fine,
        in_specs=(
            P("y", SEQ, None, None),
            P(SEQ, "y"),
            P("y", SEQ, None),
            P(None, SEQ),
            P(),
            P("y", SEQ, None),
            P("y", SEQ),
        ),
        out_specs=(P("y", SEQ, None, None), P("y", SEQ, None)),
        check_vma=False,
    )
```

```python
import jax
import jax.numpy as jnp
from jax import lax
from jax.experimental import pallas as pl
from jax.experimental.pallas import tpu as pltpu
from jax.sharding import Mesh
from jax.sharding import PartitionSpec as P

QH = 16
KH = 4
HD = 128
GROUP = QH // KH
BLOCK = 128
BASE = 10000.0
NX, NC = 4, 2
CAP = 2
SEQ = ("z", "x", "c")
XC = ("x", "c")
F32 = jnp.float32
BF = jnp.bfloat16
VM = pl.BlockSpec(memory_space=pltpu.VMEM)
SM = pl.BlockSpec(memory_space=pltpu.SMEM)
ANY = pl.BlockSpec(memory_space=pltpu.HBM)


def call(kernel, out, ins, outs, scratch=(), flops=0, moved=0, vmem=8):
    return pl.pallas_call(
        kernel,
        out_shape=out,
        in_specs=ins,
        out_specs=outs,
        scratch_shapes=list(scratch),
        compiler_params=pltpu.CompilerParams(vmem_limit_bytes=vmem << 20),
        cost_estimate=pl.CostEstimate(flops=flops, bytes_accessed=moved, transcendentals=0),
    )


def kept(*arrays):
    return [pltpu.with_memory_space_constraint(a, pltpu.HBM) for a in arrays]


def pick_kernel(owner, me, pool, one_up, one_down, two_up, two_down, three_up, three_down, stays, staged, sem, out_sem):
    traces, blocks = owner.shape
    rows = pool.shape[0] // blocks
    mine = me[0]
    for slot in range(blocks):
        stays[slot] = 0
        here = pl.ds(slot * rows, rows)
        pltpu.make_async_copy(pool.at[here], staged.at[here], sem.at[slot]).start()
    for slot in range(blocks):
        here = pl.ds(slot * rows, rows)
        pltpu.make_async_copy(pool.at[here], staged.at[here], sem.at[slot]).wait()
    slots = {
        1: (one_up.at[0], one_up.at[1]),
        2: (two_up.at[0], two_up.at[1]),
        3: (three_up.at[0], three_up.at[1]),
        4: (one_up.at[2], one_down.at[2]),
        5: (three_down.at[0], three_down.at[1]),
        6: (two_down.at[0], two_down.at[1]),
        7: (one_down.at[0], one_down.at[1]),
    }
    for d in range(traces):
        t = lax.rem(mine + d, traces)
        count = jnp.int32(0)
        for b in range(blocks):
            o = owner[t, b]
            slot = o % blocks
            hit = o // blocks == mine
            for nth in range(CAP if d else 0):

                @pl.when(hit & (count == nth))
                def _(slot=slot, out=slots[d][nth]):
                    start = pl.multiple_of(slot * rows, rows)
                    pltpu.make_async_copy(
                        staged.at[pl.ds(start, rows)], out, out_sem.at[slot]
                    ).start()

            if d == 0:

                @pl.when(hit)
                def _(slot=slot):
                    stays[slot] = 1

            count = count + hit.astype(jnp.int32)
    for slot in range(blocks):

        @pl.when(stays[slot] == 0)
        def _(slot=slot):
            pltpu.make_async_copy(
                staged.at[pl.ds(slot * rows, rows)], two_up.at[0], out_sem.at[slot]
            ).wait()


def head(ref, n):
    per = ref.shape[2] // HD
    return ref[n // per, :, pl.ds((n % per) * HD, HD)]


def rotated(x, cos, sin):
    x = x.astype(F32)
    return x * cos + pltpu.roll(x, HD // 2, 1) * sin


def rope_kernel(proj, cos, sin, sel, q_out, fresh):
    for n in range(QH):
        q_out[:, n * HD : (n + 1) * HD] = rotated(head(proj, n), cos[...], sin[...]).astype(BF)
    rows = q_out.shape[0]
    q_out[:, QH * HD :] = jnp.broadcast_to(sel[...].astype(F32), (rows, HD)).astype(BF)
    for n in range(KH):
        k = rotated(head(proj, QH + n), cos[...], sin[...])
        fresh[:, n * HD : (n + 1) * HD] = k.astype(BF)
        fresh[:, (KH + n) * HD : (KH + n + 1) * HD] = head(proj, QH + KH + n)


def attend(queries, kv, stack, masks, put):
    n_q = queries[0].shape[0]
    tokens = kv.shape[0]
    size = GROUP * n_q
    lane = lax.broadcasted_iota(jnp.int32, (n_q, HD), 1)
    sums = [jnp.zeros((n_q, HD), F32) for _ in queries]
    for k in range(KH):
        keys = kv[:, k * HD : (k + 1) * HD]
        values = kv[:, (KH + k) * HD : (KH + k + 1) * HD]
        for i, q in enumerate(queries):
            for g in range(GROUP):
                h = k * GROUP + g
                stack[i, pl.ds(g * n_q, n_q), :] = q[:, h * HD : (h + 1) * HD]
            scores = lax.dot_general(
                stack[i], keys, (((1,), (1,)), ((), ())), preferred_element_type=F32
            )
            w = jnp.exp(scores * HD ** (-0.5))
            if masks[i] is not None:
                w = jnp.where(masks[i][None], w.reshape(GROUP, n_q, tokens), 0.0)
                w = w.reshape(size, tokens)
            total = jnp.sum(w, axis=1, keepdims=True)
            num = jnp.dot(w.astype(BF), values, preferred_element_type=F32)
            for g in range(GROUP):
                h = k * GROUP + g
                here = slice(g * n_q, (g + 1) * n_q)
                sums[i] = jnp.where(lane == h, total[here], sums[i])
                put(i, pl.ds(h * HD, HD), num[here])
    return sums


def token_of(q, tokens):
    n_q = q.shape[0]
    per = n_q // (tokens // BLOCK)
    block = lax.broadcasted_iota(jnp.int32, (n_q, 1), 0) // per
    return block * BLOCK + q[:, QH * HD : QH * HD + 1].astype(F32).astype(jnp.int32)


def blend_kernel(
    owner, me, kcos, ksin, spots, fresh, q1, q2,
    pool, one_up, one_down, two_up, two_down, three_up, three_down,
    blended, p1, p2, kv, stack, sem, out_sem,
):
    traces, blocks = owner.shape
    rows = kv.shape[0] // blocks
    mine = me[0]
    own = [owner[mine, b] // blocks for b in range(blocks)]
    slots = {
        1: (one_up.at[0], one_up.at[1]),
        2: (two_up.at[0], two_up.at[1]),
        3: (three_up.at[0], three_up.at[1]),
        4: (three_up.at[2], three_down.at[2]),
        5: (three_down.at[0], three_down.at[1]),
        6: (two_down.at[0], two_down.at[1]),
        7: (one_down.at[0], one_down.at[1]),
    }
    for b in range(blocks):
        here = kv.at[pl.ds(b * rows, rows)]
        rank = jnp.int32(0)
        for e in range(b):
            rank = rank + (own[e] == own[b]).astype(jnp.int32)
        d = lax.rem(mine - own[b] + traces, traces)

        @pl.when(d == 0)
        def _(b=b, here=here):
            start = pl.multiple_of(owner[mine, b] % blocks * rows, rows)
            pltpu.make_async_copy(pool.at[pl.ds(start, rows)], here, sem.at[b]).start()

        for far in range(1, traces):
            for nth in range(CAP):

                @pl.when((d == far) & (rank == nth))
                def _(b=b, here=here, block=slots[far][nth]):
                    pltpu.make_async_copy(block, here, sem.at[b]).start()

    width = kv.shape[1]
    n_q = fresh.shape[0]
    ones = jnp.ones((n_q, HD), BF)
    for b in range(blocks):
        here = pl.ds(b * rows, rows)
        at = lax.broadcasted_iota(jnp.int32, (rows, n_q), 0) + b * rows
        hits = (at == spots[...]).astype(F32).astype(BF)
        chosen = jnp.dot(hits, ones, preferred_element_type=F32) > 0.5
        pltpu.make_async_copy(two_up.at[0], kv.at[here], sem.at[b]).wait()
        cos, sin = kcos[b : b + 1, :], ksin[b : b + 1, :]
        for n in range(width // HD):
            cols = pl.ds(n * HD, HD)
            x = kv[here, cols]
            x = rotated(x, cos, sin) if n < KH else x.astype(F32)
            placed = jnp.dot(hits, fresh[:, cols], preferred_element_type=F32)
            kv[here, cols] = jnp.where(chosen, placed, x).astype(BF)
        pltpu.make_async_copy(kv.at[here], blended.at[here], out_sem.at[b]).start()
    tokens = kv.shape[0]
    key = lax.broadcasted_iota(jnp.int32, (n_q, tokens), 1)

    def put(i, cols, num):
        (p1, p2)[i][:, cols] = num.astype(BF)

    sums = attend([q1, q2], kv, stack, [None, key > token_of(q2, tokens)], put)
    lane = lax.broadcasted_iota(jnp.int32, (n_q, HD), 1)
    for p, d in zip((p1, p2), sums):
        high = d.astype(BF)
        low = d - high.astype(F32)
        p[:, QH * HD :] = jnp.where(
            lane < QH, high.astype(F32), pltpu.roll(low, QH, 1)
        ).astype(BF)
    for b in range(blocks):
        here = pl.ds(b * rows, rows)
        pltpu.make_async_copy(kv.at[here], blended.at[here], out_sem.at[b]).wait()


def own_kernel(q0, kv, num0, den0, stack):
    tokens = kv.shape[0]
    n_q = q0.shape[0]
    key = lax.broadcasted_iota(jnp.int32, (n_q, tokens), 1)

    def put(i, cols, num):
        num0[:, cols] = num

    (den0[...],) = attend([q0], kv, stack, [key <= token_of(q0, tokens)], put)


def merge_kernel(num0, den0, r1, r2, live, out):
    total = den0[...]
    for r in (r1, r2):
        d = r[:, QH * HD :].astype(F32)
        total = total + d + pltpu.roll(d, HD - QH, 1)
    alive = live[...] > 0
    for h in range(QH):
        cols = pl.ds(h * HD, HD)
        num = num0[:, cols] + r1[:, cols].astype(F32) + r2[:, cols].astype(F32)
        out[:, cols] = jnp.where(alive, num / total[:, h : h + 1], 0.0).astype(BF)


def half_turns(angles):
    cos, sin = jnp.cos(angles), jnp.sin(angles)
    return jnp.concatenate([cos, cos], -1), jnp.concatenate([-sin, sin], -1)


def on_device(sel_hidden, w_qkv, cache_pool, block_owner, doc_lengths, sel_index, sel_count):
    ny, nz = lax.axis_size("y"), lax.axis_size("z")
    y = lax.axis_index("y")
    shard = lax.axis_index(SEQ)
    group = NX * NC
    n_seq = nz * group
    _, blocks, slots, d = sel_hidden.shape
    rows = blocks * slots
    tokens, kvw = cache_pool.shape[1:]
    block_len = tokens // blocks
    cols = w_qkv.shape[1]
    me = y.reshape(1).astype(jnp.int32)

    def turned(array, by):
        return lax.ppermute(array, "y", [(i, (i + by) % ny) for i in range(ny)])

    def room(n):
        return pltpu.HBM((n, block_len, kvw), BF)

    one_up, one_down, two_up, two_down, three_up, three_down = call(
        pick_kernel,
        (room(3), room(3), room(2), room(2), room(3), room(3)),
        [SM, SM, ANY], (ANY,) * 6,
        [
            pltpu.SMEM((blocks,), jnp.int32),
            pltpu.VMEM((tokens, kvw), BF),
            pltpu.SemaphoreType.DMA((blocks,)),
            pltpu.SemaphoreType.DMA((blocks,)),
        ],
        moved=4 * tokens * kvw,
    )(block_owner, me, *kept(cache_pool[0]))
    def crossed(m):
        pairs = [(a * group + b, (b ^ m) * group + a) for a in range(ny) for b in range(group)]
        return lax.ppermute(w_qkv, ("y", "x", "c"), pairs)

    def paired(mine, other, bit, axis):
        low = (y // bit) % 2 == 0
        return jnp.stack([jnp.where(low, mine, other), jnp.where(low, other, mine)], axis)

    w = paired(
        paired(crossed(0), crossed(4), 4, 0), paired(crossed(2), crossed(6), 4, 0), 2, 1
    )
    w = paired(w, lax.ppermute(w, "y", [(i, i ^ 1) for i in range(ny)]), 1, 2).reshape(-1, cols)
    w, one_up, one_down, two_up, two_down = lax.optimization_barrier(
        (w, one_up, one_down, two_up, two_down)
    )
    one_up, one_down = turned(one_up, 1), turned(one_down, -1)
    two_up, two_down = turned(two_up, 2), turned(two_down, -2)
    hidden = lax.all_gather(sel_hidden.reshape(rows, d), XC, axis=0, tiled=True)
    w, hidden, one_up, one_down = lax.optimization_barrier((w, hidden, one_up, one_down))
    w = lax.all_gather(w, "z", axis=0, tiled=True)
    three_up = turned(lax.dynamic_update_slice(three_up, one_up[2:], (2, 0, 0)), 3)
    three_down = turned(lax.dynamic_update_slice(three_down, one_down[2:], (2, 0, 0)), -3)
    hidden, w, two_up, two_down = lax.optimization_barrier((hidden, w, two_up, two_down))
    projected = jnp.dot(hidden, w, preferred_element_type=F32).astype(BF)
    projected = projected.reshape(group, rows, cols)
    merged = lax.all_to_all(projected, XC, 0, 0, tiled=True)

    frequency = 1.0 / BASE ** (jnp.arange(HD // 2, dtype=F32) * 2.0 / HD)
    index = jnp.arange(blocks, dtype=jnp.int32)
    local = (index[:, None] * block_len + sel_index[0]).reshape(rows)
    live = (jnp.arange(slots, dtype=jnp.int32)[None, :] < sel_count[0][:, None]).reshape(rows)
    cos, sin = half_turns((shard * tokens + local).astype(F32)[:, None] * frequency)
    lengths = lax.dynamic_index_in_dim(doc_lengths, y, 0, keepdims=False)
    nth = jnp.arange(lengths.shape[0], dtype=jnp.int32)
    ends = jnp.sum(jnp.where(nth[None, :] <= nth[:, None], lengths[None, :], 0), axis=1)
    here = shard * blocks + index
    first = jnp.sum(jnp.where(ends[None, :] <= here[:, None], lengths[None, :], 0), axis=1)
    kcos, ksin = half_turns((first * block_len).astype(F32)[:, None] * frequency)
    spots = jnp.where(live, local, -1).reshape(1, rows)

    wide = QH * HD + HD
    queries, fresh = call(
        rope_kernel,
        (jax.ShapeDtypeStruct((rows, wide), BF), jax.ShapeDtypeStruct((rows, kvw), BF)),
        [VM] * 4, (VM, VM),
        moved=4 * rows * (wide + kvw),
    )(merged, cos, sin, sel_index.reshape(rows, 1))

    def along(array, by):
        pairs = [(i, i + by) for i in range(n_seq) if 0 <= i + by < n_seq]
        return lax.ppermute(array, SEQ, pairs)

    q1, q2 = along(queries, -1), along(queries, -2)
    partial = jax.ShapeDtypeStruct((rows, wide), BF)
    blended, p1, p2 = call(
        blend_kernel,
        (pltpu.HBM((tokens, kvw), BF), partial, partial),
        [SM, SM] + [VM] * 6 + [ANY] * 7, (ANY, VM, VM),
        [
            pltpu.VMEM((tokens, kvw), BF),
            pltpu.VMEM((2, GROUP * rows, HD), BF),
            pltpu.SemaphoreType.DMA((blocks,)),
            pltpu.SemaphoreType.DMA((blocks,)),
        ],
        flops=8 * rows * QH * HD * tokens,
        moved=4 * tokens * kvw,
        vmem=24,
    )(
        block_owner, me, kcos, ksin, spots, fresh, q1, q2,
        *kept(cache_pool[0], one_up, one_down, two_up, two_down, three_up, three_down),
    )
    whole, p1, p2 = lax.optimization_barrier((blended, p1, p2))
    r1, r2 = along(p1, 1), along(p2, 2)
    num0, den0 = call(
        own_kernel,
        (jax.ShapeDtypeStruct((rows, QH * HD), F32), jax.ShapeDtypeStruct((rows, HD), F32)),
        [VM] * 2, (VM, VM),
        [pltpu.VMEM((1, GROUP * rows, HD), BF)],
        flops=4 * rows * QH * HD * tokens,
        moved=2 * tokens * kvw,
        vmem=20,
    )(queries, whole)
    attended = call(
        merge_kernel,
        jax.ShapeDtypeStruct((rows, QH * HD), BF),
        [VM] * 5, VM,
        moved=12 * rows * QH * HD,
    )(num0, den0, r1, r2, live.astype(jnp.int32).reshape(rows, 1))
    return attended.reshape(1, blocks, slots, QH * HD), blended[None]


def solution(mesh):
    ny, n_seq = mesh.devices.shape
    fine = Mesh(
        mesh.devices.reshape(ny, n_seq // (NX * NC), NX, NC), ("y", "z", "x", "c")
    )
    return jax.shard_map(
        on_device,
        mesh=fine,
        in_specs=(
            P("y", SEQ, None, None),
            P(SEQ, "y"),
            P("y", SEQ, None),
            P(None, SEQ),
            P(),
            P("y", SEQ, None),
            P("y", SEQ),
        ),
        out_specs=(P("y", SEQ, None, None), P("y", SEQ, None)),
        check_vma=False,
    )
```

```python
import jax
import jax.numpy as jnp
from jax import lax
from jax.experimental import pallas as pl
from jax.experimental.pallas import tpu as pltpu
from jax.sharding import Mesh
from jax.sharding import PartitionSpec as P

QH = 16
KH = 4
HD = 128
GROUP = QH // KH
BLOCK = 128
WIDE = 1024
BASE = 10000.0
NX, NC = 4, 2
CAP = 2
SEQ = ("z", "x", "c")
XC = ("x", "c")
F32 = jnp.float32
BF = jnp.bfloat16
VM = pl.BlockSpec(memory_space=pltpu.VMEM)
SM = pl.BlockSpec(memory_space=pltpu.SMEM)
ANY = pl.BlockSpec(memory_space=pltpu.HBM)


def call(kernel, out, ins, outs, scratch=(), flops=0, moved=0, vmem=8):
    return pl.pallas_call(
        kernel,
        out_shape=out,
        in_specs=ins,
        out_specs=outs,
        scratch_shapes=list(scratch),
        compiler_params=pltpu.CompilerParams(vmem_limit_bytes=vmem << 20),
        cost_estimate=pl.CostEstimate(flops=flops, bytes_accessed=moved, transcendentals=0),
    )


def kept(*arrays):
    return [pltpu.with_memory_space_constraint(a, pltpu.HBM) for a in arrays]


def pick_kernel(owner, me, pool, one_up, one_down, two_up, two_down, three_up, three_down, stays, staged, sem, out_sem):
    traces, blocks = owner.shape
    rows = pool.shape[0] // blocks
    mine = me[0]
    for slot in range(blocks):
        stays[slot] = 0
        here = pl.ds(slot * rows, rows)
        pltpu.make_async_copy(pool.at[here], staged.at[here], sem.at[slot]).start()
    for slot in range(blocks):
        here = pl.ds(slot * rows, rows)
        pltpu.make_async_copy(pool.at[here], staged.at[here], sem.at[slot]).wait()
    slots = {
        1: (one_up.at[pl.ds(0, rows)], one_up.at[pl.ds(rows, rows)]),
        2: (two_up.at[0], two_up.at[1]),
        3: (three_up.at[0], three_up.at[1]),
        4: (one_up.at[pl.ds(2 * rows, rows)], one_down.at[pl.ds(2 * rows, rows)]),
        5: (three_down.at[0], three_down.at[1]),
        6: (two_down.at[0], two_down.at[1]),
        7: (one_down.at[pl.ds(0, rows)], one_down.at[pl.ds(rows, rows)]),
    }
    for d in range(traces):
        t = lax.rem(mine + d, traces)
        count = jnp.int32(0)
        for b in range(blocks):
            o = owner[t, b]
            slot = o % blocks
            hit = o // blocks == mine
            for nth in range(CAP if d else 0):

                @pl.when(hit & (count == nth))
                def _(slot=slot, out=slots[d][nth]):
                    start = pl.multiple_of(slot * rows, rows)
                    pltpu.make_async_copy(
                        staged.at[pl.ds(start, rows)], out, out_sem.at[slot]
                    ).start()

            if d == 0:

                @pl.when(hit)
                def _(slot=slot):
                    stays[slot] = 1

            count = count + hit.astype(jnp.int32)
    for slot in range(blocks):

        @pl.when(stays[slot] == 0)
        def _(slot=slot):
            pltpu.make_async_copy(
                staged.at[pl.ds(slot * rows, rows)], two_up.at[0], out_sem.at[slot]
            ).wait()


def tiles(w):
    n = 0
    for part in range(w.shape[0]):
        for r in range(0, w.shape[1], 16):
            for c in range(0, w.shape[2], HD):
                at = (pl.ds(n * HD // WIDE * 16, 16), pl.ds(n * HD % WIDE, HD))
                yield at, (part, pl.ds(r, 16), pl.ds(c, HD))
                n += 1


def pack_kernel(y, e0, e2, e4, e6, up_in, down_in, up, down, w, all_w, packed, sem):
    for k, e in enumerate((e0, e2, e4, e6)):
        all_w[k] = e[...]
    for n in range(w.shape[0]):
        w[n] = all_w[n ^ (y[0] // 2)]
    for at, place in tiles(w):
        packed[at] = w[place]
    size = packed.shape[0]
    copies = [
        pltpu.make_async_copy(packed, to.at[pl.ds(to.shape[0] - size, size)], sem.at[i])
        for i, to in enumerate((up, down))
    ]
    for copy in copies:
        copy.start()
    for copy in copies:
        copy.wait()


def unpack_kernel(y, w, up, down, out, other, packed, sem):
    tail = pl.ds(up.shape[0] - packed.shape[0], packed.shape[0])
    odd = lax.rem(y[0], 2)

    @pl.when(odd == 1)
    def _():
        pltpu.make_async_copy(up.at[tail], packed, sem).start()

    @pl.when(odd == 0)
    def _():
        pltpu.make_async_copy(down.at[tail], packed, sem).start()

    for n in range(w.shape[0]):
        out[2 * n + odd] = w[n]
    pltpu.make_async_copy(up.at[tail], packed, sem).wait()
    for at, place in tiles(w):
        other[place] = packed[at]
    for n in range(w.shape[0]):
        out[2 * n + 1 - odd] = other[n]


def head(ref, n):
    per = ref.shape[2] // HD
    return ref[n // per, :, pl.ds((n % per) * HD, HD)]


def rotated(x, cos, sin):
    x = x.astype(F32)
    return x * cos + pltpu.roll(x, HD // 2, 1) * sin


def rope_kernel(proj, cos, sin, sel, q_out, fresh):
    for n in range(QH):
        q_out[:, n * HD : (n + 1) * HD] = rotated(head(proj, n), cos[...], sin[...]).astype(BF)
    rows = q_out.shape[0]
    q_out[:, QH * HD :] = jnp.broadcast_to(sel[...].astype(F32), (rows, HD)).astype(BF)
    for n in range(KH):
        k = rotated(head(proj, QH + n), cos[...], sin[...])
        fresh[:, n * HD : (n + 1) * HD] = k.astype(BF)
        fresh[:, (KH + n) * HD : (KH + n + 1) * HD] = head(proj, QH + KH + n)


def attend(queries, kv, stack, masks, put):
    n_q = queries[0].shape[0]
    tokens = kv.shape[0]
    size = GROUP * n_q
    lane = lax.broadcasted_iota(jnp.int32, (n_q, HD), 1)
    sums = [jnp.zeros((n_q, HD), F32) for _ in queries]
    for k in range(KH):
        keys = kv[:, k * HD : (k + 1) * HD]
        values = kv[:, (KH + k) * HD : (KH + k + 1) * HD]
        for i, q in enumerate(queries):
            for g in range(GROUP):
                h = k * GROUP + g
                stack[i, pl.ds(g * n_q, n_q), :] = q[:, h * HD : (h + 1) * HD]
            scores = lax.dot_general(
                stack[i], keys, (((1,), (1,)), ((), ())), preferred_element_type=F32
            )
            w = jnp.exp(scores * HD ** (-0.5))
            if masks[i] is not None:
                w = jnp.where(masks[i][None], w.reshape(GROUP, n_q, tokens), 0.0)
                w = w.reshape(size, tokens)
            total = jnp.sum(w, axis=1, keepdims=True)
            num = jnp.dot(w.astype(BF), values, preferred_element_type=F32)
            for g in range(GROUP):
                h = k * GROUP + g
                here = slice(g * n_q, (g + 1) * n_q)
                sums[i] = jnp.where(lane == h, total[here], sums[i])
                put(i, pl.ds(h * HD, HD), num[here])
    return sums


def token_of(q, tokens):
    n_q = q.shape[0]
    per = n_q // (tokens // BLOCK)
    block = lax.broadcasted_iota(jnp.int32, (n_q, 1), 0) // per
    return block * BLOCK + q[:, QH * HD : QH * HD + 1].astype(F32).astype(jnp.int32)


def blend_kernel(
    owner, me, kcos, ksin, spots, fresh, q1, q2,
    pool, one_up, one_down, two_up, two_down, three_up, three_down,
    blended, p1, p2, kv, stack, sem, out_sem,
):
    traces, blocks = owner.shape
    rows = kv.shape[0] // blocks
    mine = me[0]
    own = [owner[mine, b] // blocks for b in range(blocks)]
    slots = {
        1: (one_up.at[pl.ds(0, rows)], one_up.at[pl.ds(rows, rows)]),
        2: (two_up.at[0], two_up.at[1]),
        3: (three_up.at[0], three_up.at[1]),
        4: (three_up.at[2], three_down.at[2]),
        5: (three_down.at[0], three_down.at[1]),
        6: (two_down.at[0], two_down.at[1]),
        7: (one_down.at[pl.ds(0, rows)], one_down.at[pl.ds(rows, rows)]),
    }
    for b in range(blocks):
        here = kv.at[pl.ds(b * rows, rows)]
        rank = jnp.int32(0)
        for e in range(b):
            rank = rank + (own[e] == own[b]).astype(jnp.int32)
        d = lax.rem(mine - own[b] + traces, traces)

        @pl.when(d == 0)
        def _(b=b, here=here):
            start = pl.multiple_of(owner[mine, b] % blocks * rows, rows)
            pltpu.make_async_copy(pool.at[pl.ds(start, rows)], here, sem.at[b]).start()

        for far in range(1, traces):
            for nth in range(CAP):

                @pl.when((d == far) & (rank == nth))
                def _(b=b, here=here, block=slots[far][nth]):
                    pltpu.make_async_copy(block, here, sem.at[b]).start()

    width = kv.shape[1]
    n_q = fresh.shape[0]
    ones = jnp.ones((n_q, HD), BF)
    for b in range(blocks):
        here = pl.ds(b * rows, rows)
        at = lax.broadcasted_iota(jnp.int32, (rows, n_q), 0) + b * rows
        hits = (at == spots[...]).astype(F32).astype(BF)
        chosen = jnp.dot(hits, ones, preferred_element_type=F32) > 0.5
        pltpu.make_async_copy(two_up.at[0], kv.at[here], sem.at[b]).wait()
        cos, sin = kcos[b : b + 1, :], ksin[b : b + 1, :]
        for n in range(width // HD):
            cols = pl.ds(n * HD, HD)
            x = kv[here, cols]
            x = rotated(x, cos, sin) if n < KH else x.astype(F32)
            placed = jnp.dot(hits, fresh[:, cols], preferred_element_type=F32)
            kv[here, cols] = jnp.where(chosen, placed, x).astype(BF)
        pltpu.make_async_copy(kv.at[here], blended.at[here], out_sem.at[b]).start()
    tokens = kv.shape[0]
    key = lax.broadcasted_iota(jnp.int32, (n_q, tokens), 1)

    def put(i, cols, num):
        (p1, p2)[i][:, cols] = num.astype(BF)

    sums = attend([q1, q2], kv, stack, [None, key > token_of(q2, tokens)], put)
    lane = lax.broadcasted_iota(jnp.int32, (n_q, HD), 1)
    for p, d in zip((p1, p2), sums):
        high = d.astype(BF)
        low = d - high.astype(F32)
        p[:, QH * HD :] = jnp.where(
            lane < QH, high.astype(F32), pltpu.roll(low, QH, 1)
        ).astype(BF)
    for b in range(blocks):
        here = pl.ds(b * rows, rows)
        pltpu.make_async_copy(kv.at[here], blended.at[here], out_sem.at[b]).wait()


def own_kernel(q0, kv, num0, den0, stack):
    tokens = kv.shape[0]
    n_q = q0.shape[0]
    key = lax.broadcasted_iota(jnp.int32, (n_q, tokens), 1)

    def put(i, cols, num):
        num0[:, cols] = num

    (den0[...],) = attend([q0], kv, stack, [key <= token_of(q0, tokens)], put)


def merge_kernel(num0, den0, r1, r2, live, out):
    total = den0[...]
    for r in (r1, r2):
        d = r[:, QH * HD :].astype(F32)
        total = total + d + pltpu.roll(d, HD - QH, 1)
    alive = live[...] > 0
    for h in range(QH):
        cols = pl.ds(h * HD, HD)
        num = num0[:, cols] + r1[:, cols].astype(F32) + r2[:, cols].astype(F32)
        out[:, cols] = jnp.where(alive, num / total[:, h : h + 1], 0.0).astype(BF)


def half_turns(angles):
    cos, sin = jnp.cos(angles), jnp.sin(angles)
    return jnp.concatenate([cos, cos], -1), jnp.concatenate([-sin, sin], -1)


def on_device(sel_hidden, w_qkv, cache_pool, block_owner, doc_lengths, sel_index, sel_count):
    ny, nz = lax.axis_size("y"), lax.axis_size("z")
    y = lax.axis_index("y")
    shard = lax.axis_index(SEQ)
    group = NX * NC
    n_seq = nz * group
    _, blocks, slots, d = sel_hidden.shape
    rows = blocks * slots
    tokens, kvw = cache_pool.shape[1:]
    block_len = tokens // blocks
    cols = w_qkv.shape[1]
    me = y.reshape(1).astype(jnp.int32)

    def turned(array, by):
        return lax.ppermute(array, "y", [(i, (i + by) % ny) for i in range(ny)])

    tail = 4 * w_qkv.size // kvw
    tall = 3 * block_len + tail

    def room(n):
        return pltpu.HBM((n, block_len, kvw), BF)

    one_up, one_down, two_up, two_down, three_up, three_down = call(
        pick_kernel,
        (pltpu.HBM((tall, kvw), BF),) * 2 + (room(2), room(2), room(3), room(3)),
        [SM, SM, ANY], (ANY,) * 6,
        [
            pltpu.SMEM((blocks,), jnp.int32),
            pltpu.VMEM((tokens, kvw), BF),
            pltpu.SemaphoreType.DMA((blocks,)),
            pltpu.SemaphoreType.DMA((blocks,)),
        ],
        moved=4 * tokens * kvw,
    )(block_owner, me, *kept(cache_pool[0]))
    def crossed(m):
        pairs = [(a * group + b, (b ^ m) * group + a) for a in range(ny) for b in range(group)]
        return lax.ppermute(w_qkv, ("y", "x", "c"), pairs)

    one_up, one_down, w = pl.pallas_call(
        pack_kernel,
        out_shape=(
            pltpu.HBM((tall, kvw), BF),
            pltpu.HBM((tall, kvw), BF),
            jax.ShapeDtypeStruct((4,) + w_qkv.shape, BF),
        ),
        in_specs=[SM] + [VM] * 4 + [ANY] * 2,
        out_specs=(ANY, ANY, VM),
        scratch_shapes=[
            pltpu.VMEM((4,) + w_qkv.shape, BF),
            pltpu.VMEM((tail, kvw), BF),
            pltpu.SemaphoreType.DMA((2,)),
        ],
        input_output_aliases={5: 0, 6: 1},
        compiler_params=pltpu.CompilerParams(vmem_limit_bytes=8 << 20),
    )(me, crossed(0), crossed(2), crossed(4), crossed(6), *kept(one_up, one_down))
    one_up, one_down = turned(one_up, 1), turned(one_down, -1)
    w = call(
        unpack_kernel,
        jax.ShapeDtypeStruct((8,) + w_qkv.shape, BF),
        [SM, VM] + [pl.BlockSpec(memory_space=pl.ANY)] * 2, VM,
        [
            pltpu.VMEM((4,) + w_qkv.shape, BF),
            pltpu.VMEM((tail, kvw), BF),
            pltpu.SemaphoreType.DMA,
        ],
        moved=8 * w_qkv.size,
    )(me, w, one_up, one_down).reshape(-1, cols)
    w, two_up, two_down = lax.optimization_barrier((w, two_up, two_down))
    two_up, two_down = turned(two_up, 2), turned(two_down, -2)
    hidden = lax.all_gather(sel_hidden.reshape(rows, d), XC, axis=0, tiled=True)
    w, hidden = lax.optimization_barrier((w, hidden))
    w = lax.all_gather(w, "z", axis=0, tiled=True)
    three_up = turned(lax.dynamic_update_slice(three_up, one_up[2 * block_len : 3 * block_len][None], (2, 0, 0)), 3)
    three_down = turned(lax.dynamic_update_slice(three_down, one_down[2 * block_len : 3 * block_len][None], (2, 0, 0)), -3)
    hidden, w, two_up, two_down = lax.optimization_barrier((hidden, w, two_up, two_down))
    projected = jnp.dot(hidden, w, preferred_element_type=F32).astype(BF)
    projected = projected.reshape(group, rows, cols)
    merged = lax.all_to_all(projected, XC, 0, 0, tiled=True)

    frequency = 1.0 / BASE ** (jnp.arange(HD // 2, dtype=F32) * 2.0 / HD)
    index = jnp.arange(blocks, dtype=jnp.int32)
    local = (index[:, None] * block_len + sel_index[0]).reshape(rows)
    live = (jnp.arange(slots, dtype=jnp.int32)[None, :] < sel_count[0][:, None]).reshape(rows)
    cos, sin = half_turns((shard * tokens + local).astype(F32)[:, None] * frequency)
    lengths = lax.dynamic_index_in_dim(doc_lengths, y, 0, keepdims=False)
    nth = jnp.arange(lengths.shape[0], dtype=jnp.int32)
    ends = jnp.sum(jnp.where(nth[None, :] <= nth[:, None], lengths[None, :], 0), axis=1)
    here = shard * blocks + index
    first = jnp.sum(jnp.where(ends[None, :] <= here[:, None], lengths[None, :], 0), axis=1)
    kcos, ksin = half_turns((first * block_len).astype(F32)[:, None] * frequency)
    spots = jnp.where(live, local, -1).reshape(1, rows)

    wide = QH * HD + HD
    queries, fresh = call(
        rope_kernel,
        (jax.ShapeDtypeStruct((rows, wide), BF), jax.ShapeDtypeStruct((rows, kvw), BF)),
        [VM] * 4, (VM, VM),
        moved=4 * rows * (wide + kvw),
    )(merged, cos, sin, sel_index.reshape(rows, 1))

    def along(array, by):
        pairs = [(i, i + by) for i in range(n_seq) if 0 <= i + by < n_seq]
        return lax.ppermute(array, SEQ, pairs)

    q1, q2 = along(queries, -1), along(queries, -2)
    partial = jax.ShapeDtypeStruct((rows, wide), BF)
    blended, p1, p2 = call(
        blend_kernel,
        (pltpu.HBM((tokens, kvw), BF), partial, partial),
        [SM, SM] + [VM] * 6 + [ANY] * 7, (ANY, VM, VM),
        [
            pltpu.VMEM((tokens, kvw), BF),
            pltpu.VMEM((2, GROUP * rows, HD), BF),
            pltpu.SemaphoreType.DMA((blocks,)),
            pltpu.SemaphoreType.DMA((blocks,)),
        ],
        flops=8 * rows * QH * HD * tokens,
        moved=4 * tokens * kvw,
        vmem=24,
    )(
        block_owner, me, kcos, ksin, spots, fresh, q1, q2,
        *kept(cache_pool[0], one_up, one_down, two_up, two_down, three_up, three_down),
    )
    whole, p1, p2 = lax.optimization_barrier((blended, p1, p2))
    r1, r2 = along(p1, 1), along(p2, 2)
    num0, den0 = call(
        own_kernel,
        (jax.ShapeDtypeStruct((rows, QH * HD), F32), jax.ShapeDtypeStruct((rows, HD), F32)),
        [VM] * 2, (VM, VM),
        [pltpu.VMEM((1, GROUP * rows, HD), BF)],
        flops=4 * rows * QH * HD * tokens,
        moved=2 * tokens * kvw,
        vmem=20,
    )(queries, whole)
    attended = call(
        merge_kernel,
        jax.ShapeDtypeStruct((rows, QH * HD), BF),
        [VM] * 5, VM,
        moved=12 * rows * QH * HD,
    )(num0, den0, r1, r2, live.astype(jnp.int32).reshape(rows, 1))
    return attended.reshape(1, blocks, slots, QH * HD), blended[None]


def solution(mesh):
    ny, n_seq = mesh.devices.shape
    fine = Mesh(
        mesh.devices.reshape(ny, n_seq // (NX * NC), NX, NC), ("y", "z", "x", "c")
    )
    return jax.shard_map(
        on_device,
        mesh=fine,
        in_specs=(
            P("y", SEQ, None, None),
            P(SEQ, "y"),
            P("y", SEQ, None),
            P(None, SEQ),
            P(),
            P("y", SEQ, None),
            P("y", SEQ),
        ),
        out_specs=(P("y", SEQ, None, None), P("y", SEQ, None)),
        check_vma=False,
    )
```

```python
import jax
import jax.numpy as jnp
from jax import lax
from jax.experimental import pallas as pl
from jax.experimental.pallas import tpu as pltpu
from jax.sharding import Mesh
from jax.sharding import PartitionSpec as P

QH = 16
KH = 4
HD = 128
GROUP = QH // KH
BLOCK = 128
BASE = 10000.0
NX, NC = 4, 2
CAP = 2
SEQ = ("z", "x", "c")
XC = ("x", "c")
F32 = jnp.float32
BF = jnp.bfloat16
VM = pl.BlockSpec(memory_space=pltpu.VMEM)
SM = pl.BlockSpec(memory_space=pltpu.SMEM)
ANY = pl.BlockSpec(memory_space=pltpu.HBM)


def call(kernel, out, ins, outs, scratch=(), flops=0, moved=0, vmem=8):
    return pl.pallas_call(
        kernel,
        out_shape=out,
        in_specs=ins,
        out_specs=outs,
        scratch_shapes=list(scratch),
        compiler_params=pltpu.CompilerParams(vmem_limit_bytes=vmem << 20),
        cost_estimate=pl.CostEstimate(flops=flops, bytes_accessed=moved, transcendentals=0),
    )


def kept(*arrays):
    return [pltpu.with_memory_space_constraint(a, pltpu.HBM) for a in arrays]


def pick_kernel(owner, me, pool, one_up, one_down, two_up, two_down, three_up, three_down, stays, staged, sem, out_sem):
    traces, blocks = owner.shape
    rows = pool.shape[0] // blocks
    mine = me[0]
    for slot in range(blocks):
        stays[slot] = 0
        here = pl.ds(slot * rows, rows)
        pltpu.make_async_copy(pool.at[here], staged.at[here], sem.at[slot]).start()
    for slot in range(blocks):
        here = pl.ds(slot * rows, rows)
        pltpu.make_async_copy(pool.at[here], staged.at[here], sem.at[slot]).wait()
    slots = {
        1: (one_up.at[0], one_up.at[1]),
        2: (two_up.at[0], two_up.at[1]),
        3: (three_up.at[0], three_up.at[1]),
        4: (one_up.at[2], one_down.at[2]),
        5: (three_down.at[0], three_down.at[1]),
        6: (two_down.at[0], two_down.at[1]),
        7: (one_down.at[0], one_down.at[1]),
    }
    for d in range(traces):
        t = lax.rem(mine + d, traces)
        count = jnp.int32(0)
        for b in range(blocks):
            o = owner[t, b]
            slot = o % blocks
            hit = o // blocks == mine
            for nth in range(CAP if d else 0):

                @pl.when(hit & (count == nth))
                def _(slot=slot, out=slots[d][nth]):
                    start = pl.multiple_of(slot * rows, rows)
                    pltpu.make_async_copy(
                        staged.at[pl.ds(start, rows)], out, out_sem.at[slot]
                    ).start()

            if d == 0:

                @pl.when(hit)
                def _(slot=slot):
                    stays[slot] = 1

            count = count + hit.astype(jnp.int32)
    for slot in range(blocks):

        @pl.when(stays[slot] == 0)
        def _(slot=slot):
            pltpu.make_async_copy(
                staged.at[pl.ds(slot * rows, rows)], two_up.at[0], out_sem.at[slot]
            ).wait()


def head(ref, n):
    per = ref.shape[2] // HD
    return ref[n // per, :, pl.ds((n % per) * HD, HD)]


def rotated(x, cos, sin):
    x = x.astype(F32)
    return x * cos + pltpu.roll(x, HD // 2, 1) * sin


def rope_kernel(proj, cos, sin, sel, q_out, fresh):
    for n in range(QH):
        q_out[:, n * HD : (n + 1) * HD] = rotated(head(proj, n), cos[...], sin[...]).astype(BF)
    rows = q_out.shape[0]
    q_out[:, QH * HD :] = jnp.broadcast_to(sel[...].astype(F32), (rows, HD)).astype(BF)
    for n in range(KH):
        k = rotated(head(proj, QH + n), cos[...], sin[...])
        fresh[:, n * HD : (n + 1) * HD] = k.astype(BF)
        fresh[:, (KH + n) * HD : (KH + n + 1) * HD] = head(proj, QH + KH + n)


def attend(queries, kv, stack, masks, put):
    n_q = queries[0].shape[0]
    tokens = kv.shape[0]
    size = GROUP * n_q
    lane = lax.broadcasted_iota(jnp.int32, (n_q, HD), 1)
    sums = [jnp.zeros((n_q, HD), F32) for _ in queries]
    for k in range(KH):
        keys = kv[:, k * HD : (k + 1) * HD]
        values = kv[:, (KH + k) * HD : (KH + k + 1) * HD]
        for i, q in enumerate(queries):
            for g in range(GROUP):
                h = k * GROUP + g
                stack[i, pl.ds(g * n_q, n_q), :] = q[:, h * HD : (h + 1) * HD]
            scores = lax.dot_general(
                stack[i], keys, (((1,), (1,)), ((), ())), preferred_element_type=F32
            )
            w = jnp.exp(scores * HD ** (-0.5))
            if masks[i] is not None:
                w = jnp.where(masks[i][None], w.reshape(GROUP, n_q, tokens), 0.0)
                w = w.reshape(size, tokens)
            total = jnp.sum(w, axis=1, keepdims=True)
            num = jnp.dot(w.astype(BF), values, preferred_element_type=F32)
            for g in range(GROUP):
                h = k * GROUP + g
                here = slice(g * n_q, (g + 1) * n_q)
                sums[i] = jnp.where(lane == h, total[here], sums[i])
                put(i, pl.ds(h * HD, HD), num[here])
    return sums


def token_of(q, tokens):
    n_q = q.shape[0]
    per = n_q // (tokens // BLOCK)
    block = lax.broadcasted_iota(jnp.int32, (n_q, 1), 0) // per
    return block * BLOCK + q[:, QH * HD : QH * HD + 1].astype(F32).astype(jnp.int32)


def blend_kernel(
    owner, me, kcos, ksin, spots, fresh, q1, q2,
    pool, one_up, one_down, two_up, two_down, three_up, three_down,
    blended, p1, p2, kv, stack, sem, out_sem,
):
    traces, blocks = owner.shape
    rows = kv.shape[0] // blocks
    mine = me[0]
    own = [owner[mine, b] // blocks for b in range(blocks)]
    slots = {
        1: (one_up.at[0], one_up.at[1]),
        2: (two_up.at[0], two_up.at[1]),
        3: (three_up.at[0], three_up.at[1]),
        4: (three_up.at[2], three_down.at[2]),
        5: (three_down.at[0], three_down.at[1]),
        6: (two_down.at[0], two_down.at[1]),
        7: (one_down.at[0], one_down.at[1]),
    }
    for b in range(blocks):
        here = kv.at[pl.ds(b * rows, rows)]
        rank = jnp.int32(0)
        for e in range(b):
            rank = rank + (own[e] == own[b]).astype(jnp.int32)
        d = lax.rem(mine - own[b] + traces, traces)

        @pl.when(d == 0)
        def _(b=b, here=here):
            start = pl.multiple_of(owner[mine, b] % blocks * rows, rows)
            pltpu.make_async_copy(pool.at[pl.ds(start, rows)], here, sem.at[b]).start()

        for far in range(1, traces):
            for nth in range(CAP):

                @pl.when((d == far) & (rank == nth))
                def _(b=b, here=here, block=slots[far][nth]):
                    pltpu.make_async_copy(block, here, sem.at[b]).start()

    width = kv.shape[1]
    n_q = fresh.shape[0]
    ones = jnp.ones((n_q, HD), BF)
    for b in range(blocks):
        here = pl.ds(b * rows, rows)
        at = lax.broadcasted_iota(jnp.int32, (rows, n_q), 0) + b * rows
        hits = (at == spots[...]).astype(F32).astype(BF)
        chosen = jnp.dot(hits, ones, preferred_element_type=F32) > 0.5
        pltpu.make_async_copy(two_up.at[0], kv.at[here], sem.at[b]).wait()
        cos, sin = kcos[b : b + 1, :], ksin[b : b + 1, :]
        for n in range(width // HD):
            cols = pl.ds(n * HD, HD)
            x = kv[here, cols]
            x = rotated(x, cos, sin) if n < KH else x.astype(F32)
            placed = jnp.dot(hits, fresh[:, cols], preferred_element_type=F32)
            kv[here, cols] = jnp.where(chosen, placed, x).astype(BF)
        pltpu.make_async_copy(kv.at[here], blended.at[here], out_sem.at[b]).start()
    tokens = kv.shape[0]
    key = lax.broadcasted_iota(jnp.int32, (n_q, tokens), 1)

    def put(i, cols, num):
        (p1, p2)[i][:, cols] = num.astype(BF)

    sums = attend([q1, q2], kv, stack, [None, key > token_of(q2, tokens)], put)
    lane = lax.broadcasted_iota(jnp.int32, (n_q, HD), 1)
    for p, d in zip((p1, p2), sums):
        high = d.astype(BF)
        low = d - high.astype(F32)
        p[:, QH * HD :] = jnp.where(
            lane < QH, high.astype(F32), pltpu.roll(low, QH, 1)
        ).astype(BF)
    for b in range(blocks):
        here = pl.ds(b * rows, rows)
        pltpu.make_async_copy(kv.at[here], blended.at[here], out_sem.at[b]).wait()


def own_kernel(q0, kv, num0, den0, stack):
    tokens = kv.shape[0]
    n_q = q0.shape[0]
    key = lax.broadcasted_iota(jnp.int32, (n_q, tokens), 1)

    def put(i, cols, num):
        num0[:, cols] = num

    (den0[...],) = attend([q0], kv, stack, [key <= token_of(q0, tokens)], put)


def merge_kernel(num0, den0, r1, r2, live, out):
    total = den0[...]
    for r in (r1, r2):
        d = r[:, QH * HD :].astype(F32)
        total = total + d + pltpu.roll(d, HD - QH, 1)
    alive = live[...] > 0
    for h in range(QH):
        cols = pl.ds(h * HD, HD)
        num = num0[:, cols] + r1[:, cols].astype(F32) + r2[:, cols].astype(F32)
        out[:, cols] = jnp.where(alive, num / total[:, h : h + 1], 0.0).astype(BF)


def half_turns(angles):
    cos, sin = jnp.cos(angles), jnp.sin(angles)
    return jnp.concatenate([cos, cos], -1), jnp.concatenate([-sin, sin], -1)


def on_device(sel_hidden, w_qkv, cache_pool, block_owner, doc_lengths, sel_index, sel_count):
    ny, nz = lax.axis_size("y"), lax.axis_size("z")
    y = lax.axis_index("y")
    shard = lax.axis_index(SEQ)
    group = NX * NC
    n_seq = nz * group
    _, blocks, slots, d = sel_hidden.shape
    rows = blocks * slots
    tokens, kvw = cache_pool.shape[1:]
    block_len = tokens // blocks
    cols = w_qkv.shape[1]
    me = y.reshape(1).astype(jnp.int32)

    def turned(array, by):
        return lax.ppermute(array, "y", [(i, (i + by) % ny) for i in range(ny)])

    def room(n):
        return pltpu.HBM((n, block_len, kvw), BF)

    one_up, one_down, two_up, two_down, three_up, three_down = call(
        pick_kernel,
        (room(3), room(3), room(2), room(2), room(3), room(3)),
        [SM, SM, ANY], (ANY,) * 6,
        [
            pltpu.SMEM((blocks,), jnp.int32),
            pltpu.VMEM((tokens, kvw), BF),
            pltpu.SemaphoreType.DMA((blocks,)),
            pltpu.SemaphoreType.DMA((blocks,)),
        ],
        moved=4 * tokens * kvw,
    )(block_owner, me, *kept(cache_pool[0]))
    one_up, w_qkv = lax.optimization_barrier((one_up, w_qkv))
    one_up, one_down = turned(one_up, 1), turned(one_down, -1)

    def crossed(m):
        pairs = [(a * group + b, (b ^ m) * group + a) for a in range(ny) for b in range(group)]
        return lax.ppermute(w_qkv, ("y", "x", "c"), pairs)

    def paired(mine, other, bit, axis):
        low = (y // bit) % 2 == 0
        return jnp.stack([jnp.where(low, mine, other), jnp.where(low, other, mine)], axis)

    w = paired(
        paired(crossed(0), crossed(4), 4, 0), paired(crossed(2), crossed(6), 4, 0), 2, 1
    )
    w, one_up, one_down = lax.optimization_barrier((w, one_up, one_down))
    w = paired(w, lax.ppermute(w, "y", [(i, i ^ 1) for i in range(ny)]), 1, 2).reshape(-1, cols)
    w, two_up, two_down, one_up, one_down = lax.optimization_barrier(
        (w, two_up, two_down, one_up, one_down)
    )
    two_up, two_down = turned(two_up, 2), turned(two_down, -2)
    hidden = lax.all_gather(sel_hidden.reshape(rows, d), XC, axis=0, tiled=True)
    w, hidden = lax.optimization_barrier((w, hidden))
    w = lax.all_gather(w, "z", axis=0, tiled=True)
    three_up = turned(lax.dynamic_update_slice(three_up, one_up[2:], (2, 0, 0)), 3)
    three_down = turned(lax.dynamic_update_slice(three_down, one_down[2:], (2, 0, 0)), -3)
    hidden, w, two_up, two_down = lax.optimization_barrier((hidden, w, two_up, two_down))
    projected = jnp.dot(hidden, w, preferred_element_type=F32).astype(BF)
    projected = projected.reshape(group, rows, cols)
    merged = lax.all_to_all(projected, XC, 0, 0, tiled=True)

    frequency = 1.0 / BASE ** (jnp.arange(HD // 2, dtype=F32) * 2.0 / HD)
    index = jnp.arange(blocks, dtype=jnp.int32)
    local = (index[:, None] * block_len + sel_index[0]).reshape(rows)
    live = (jnp.arange(slots, dtype=jnp.int32)[None, :] < sel_count[0][:, None]).reshape(rows)
    cos, sin = half_turns((shard * tokens + local).astype(F32)[:, None] * frequency)
    lengths = lax.dynamic_index_in_dim(doc_lengths, y, 0, keepdims=False)
    nth = jnp.arange(lengths.shape[0], dtype=jnp.int32)
    ends = jnp.sum(jnp.where(nth[None, :] <= nth[:, None], lengths[None, :], 0), axis=1)
    here = shard * blocks + index
    first = jnp.sum(jnp.where(ends[None, :] <= here[:, None], lengths[None, :], 0), axis=1)
    kcos, ksin = half_turns((first * block_len).astype(F32)[:, None] * frequency)
    spots = jnp.where(live, local, -1).reshape(1, rows)

    wide = QH * HD + HD
    queries, fresh = call(
        rope_kernel,
        (jax.ShapeDtypeStruct((rows, wide), BF), jax.ShapeDtypeStruct((rows, kvw), BF)),
        [VM] * 4, (VM, VM),
        moved=4 * rows * (wide + kvw),
    )(merged, cos, sin, sel_index.reshape(rows, 1))

    def along(array, by):
        pairs = [(i, i + by) for i in range(n_seq) if 0 <= i + by < n_seq]
        return lax.ppermute(array, SEQ, pairs)

    q1, q2 = along(queries, -1), along(queries, -2)
    partial = jax.ShapeDtypeStruct((rows, wide), BF)
    blended, p1, p2 = call(
        blend_kernel,
        (pltpu.HBM((tokens, kvw), BF), partial, partial),
        [SM, SM] + [VM] * 6 + [ANY] * 7, (ANY, VM, VM),
        [
            pltpu.VMEM((tokens, kvw), BF),
            pltpu.VMEM((2, GROUP * rows, HD), BF),
            pltpu.SemaphoreType.DMA((blocks,)),
            pltpu.SemaphoreType.DMA((blocks,)),
        ],
        flops=8 * rows * QH * HD * tokens,
        moved=4 * tokens * kvw,
        vmem=24,
    )(
        block_owner, me, kcos, ksin, spots, fresh, q1, q2,
        *kept(cache_pool[0], one_up, one_down, two_up, two_down, three_up, three_down),
    )
    whole, p1, p2 = lax.optimization_barrier((blended, p1, p2))
    r1, r2 = along(p1, 1), along(p2, 2)
    num0, den0 = call(
        own_kernel,
        (jax.ShapeDtypeStruct((rows, QH * HD), F32), jax.ShapeDtypeStruct((rows, HD), F32)),
        [VM] * 2, (VM, VM),
        [pltpu.VMEM((1, GROUP * rows, HD), BF)],
        flops=4 * rows * QH * HD * tokens,
        moved=2 * tokens * kvw,
        vmem=20,
    )(queries, whole)
    attended = call(
        merge_kernel,
        jax.ShapeDtypeStruct((rows, QH * HD), BF),
        [VM] * 5, VM,
        moved=12 * rows * QH * HD,
    )(num0, den0, r1, r2, live.astype(jnp.int32).reshape(rows, 1))
    return attended.reshape(1, blocks, slots, QH * HD), blended[None]


def solution(mesh):
    ny, n_seq = mesh.devices.shape
    fine = Mesh(
        mesh.devices.reshape(ny, n_seq // (NX * NC), NX, NC), ("y", "z", "x", "c")
    )
    return jax.shard_map(
        on_device,
        mesh=fine,
        in_specs=(
            P("y", SEQ, None, None),
            P(SEQ, "y"),
            P("y", SEQ, None),
            P(None, SEQ),
            P(),
            P("y", SEQ, None),
            P("y", SEQ),
        ),
        out_specs=(P("y", SEQ, None, None), P("y", SEQ, None)),
        check_vma=False,
    )
```

```python
import jax
import jax.numpy as jnp
from jax import lax
from jax.experimental import pallas as pl
from jax.experimental.pallas import tpu as pltpu
from jax.sharding import Mesh
from jax.sharding import PartitionSpec as P

QH = 16
KH = 4
HD = 128
GROUP = QH // KH
BLOCK = 128
BASE = 10000.0
NX, NC = 4, 2
CAP = 2
SEQ = ("z", "x", "c")
XC = ("x", "c")
F32 = jnp.float32
BF = jnp.bfloat16
VM = pl.BlockSpec(memory_space=pltpu.VMEM)
SM = pl.BlockSpec(memory_space=pltpu.SMEM)
ANY = pl.BlockSpec(memory_space=pltpu.HBM)


def call(kernel, out, ins, outs, scratch=(), flops=0, moved=0, vmem=8):
    return pl.pallas_call(
        kernel,
        out_shape=out,
        in_specs=ins,
        out_specs=outs,
        scratch_shapes=list(scratch),
        compiler_params=pltpu.CompilerParams(vmem_limit_bytes=vmem << 20),
        cost_estimate=pl.CostEstimate(flops=flops, bytes_accessed=moved, transcendentals=0),
    )


def kept(*arrays):
    return [pltpu.with_memory_space_constraint(a, pltpu.HBM) for a in arrays]


def pick_kernel(owner, me, pool, one_up, one_down, two_up, two_down, three_up, three_down, stays, staged, sem, out_sem):
    traces, blocks = owner.shape
    rows = pool.shape[0] // blocks
    mine = me[0]
    for slot in range(blocks):
        stays[slot] = 0
        here = pl.ds(slot * rows, rows)
        pltpu.make_async_copy(pool.at[here], staged.at[here], sem.at[slot]).start()
    for slot in range(blocks):
        here = pl.ds(slot * rows, rows)
        pltpu.make_async_copy(pool.at[here], staged.at[here], sem.at[slot]).wait()
    slots = {
        1: (one_up.at[0], one_up.at[1]),
        2: (two_up.at[0], two_up.at[1]),
        3: (three_up.at[0], three_up.at[1]),
        4: (one_up.at[2], one_down.at[2]),
        5: (three_down.at[0], three_down.at[1]),
        6: (two_down.at[0], two_down.at[1]),
        7: (one_down.at[0], one_down.at[1]),
    }
    for d in range(traces):
        t = lax.rem(mine + d, traces)
        count = jnp.int32(0)
        for b in range(blocks):
            o = owner[t, b]
            slot = o % blocks
            hit = o // blocks == mine
            for nth in range(CAP if d else 0):

                @pl.when(hit & (count == nth))
                def _(slot=slot, out=slots[d][nth]):
                    start = pl.multiple_of(slot * rows, rows)
                    pltpu.make_async_copy(
                        staged.at[pl.ds(start, rows)], out, out_sem.at[slot]
                    ).start()

            if d == 0:

                @pl.when(hit)
                def _(slot=slot):
                    stays[slot] = 1

            count = count + hit.astype(jnp.int32)
    for slot in range(blocks):

        @pl.when(stays[slot] == 0)
        def _(slot=slot):
            pltpu.make_async_copy(
                staged.at[pl.ds(slot * rows, rows)], two_up.at[0], out_sem.at[slot]
            ).wait()


def head(ref, n):
    per = ref.shape[2] // HD
    return ref[n // per, :, pl.ds((n % per) * HD, HD)]


def rotated(x, cos, sin):
    x = x.astype(F32)
    return x * cos + pltpu.roll(x, HD // 2, 1) * sin


def rope_kernel(proj, cos, sin, sel, q_out, fresh):
    for n in range(QH):
        q_out[:, n * HD : (n + 1) * HD] = rotated(head(proj, n), cos[...], sin[...]).astype(BF)
    rows = q_out.shape[0]
    q_out[:, QH * HD :] = jnp.broadcast_to(sel[...].astype(F32), (rows, HD)).astype(BF)
    for n in range(KH):
        k = rotated(head(proj, QH + n), cos[...], sin[...])
        fresh[:, n * HD : (n + 1) * HD] = k.astype(BF)
        fresh[:, (KH + n) * HD : (KH + n + 1) * HD] = head(proj, QH + KH + n)


def attend(queries, kv, stack, masks, put):
    n_q = queries[0].shape[0]
    tokens = kv.shape[0]
    size = GROUP * n_q
    lane = lax.broadcasted_iota(jnp.int32, (n_q, HD), 1)
    sums = [jnp.zeros((n_q, HD), F32) for _ in queries]
    for k in range(KH):
        keys = kv[:, k * HD : (k + 1) * HD]
        values = kv[:, (KH + k) * HD : (KH + k + 1) * HD]
        for i, q in enumerate(queries):
            for g in range(GROUP):
                h = k * GROUP + g
                stack[i, pl.ds(g * n_q, n_q), :] = q[:, h * HD : (h + 1) * HD]
            scores = lax.dot_general(
                stack[i], keys, (((1,), (1,)), ((), ())), preferred_element_type=F32
            )
            w = jnp.exp(scores * HD ** (-0.5))
            if masks[i] is not None:
                w = jnp.where(masks[i][None], w.reshape(GROUP, n_q, tokens), 0.0)
                w = w.reshape(size, tokens)
            total = jnp.sum(w, axis=1, keepdims=True)
            num = jnp.dot(w.astype(BF), values, preferred_element_type=F32)
            for g in range(GROUP):
                h = k * GROUP + g
                here = slice(g * n_q, (g + 1) * n_q)
                sums[i] = jnp.where(lane == h, total[here], sums[i])
                put(i, pl.ds(h * HD, HD), num[here])
    return sums


def token_of(q, tokens):
    n_q = q.shape[0]
    per = n_q // (tokens // BLOCK)
    block = lax.broadcasted_iota(jnp.int32, (n_q, 1), 0) // per
    return block * BLOCK + q[:, QH * HD : QH * HD + 1].astype(F32).astype(jnp.int32)


def blend_kernel(
    owner, me, kcos, ksin, spots, fresh,
    pool, one_up, one_down, two_up, two_down, three_up, three_down,
    blended, kv, sem, out_sem,
):
    traces, blocks = owner.shape
    rows = kv.shape[0] // blocks
    mine = me[0]
    own = [owner[mine, b] // blocks for b in range(blocks)]
    slots = {
        1: (one_up.at[0], one_up.at[1]),
        2: (two_up.at[0], two_up.at[1]),
        3: (three_up.at[0], three_up.at[1]),
        4: (three_up.at[2], three_down.at[2]),
        5: (three_down.at[0], three_down.at[1]),
        6: (two_down.at[0], two_down.at[1]),
        7: (one_down.at[0], one_down.at[1]),
    }
    for b in range(blocks):
        here = kv.at[pl.ds(b * rows, rows)]
        rank = jnp.int32(0)
        for e in range(b):
            rank = rank + (own[e] == own[b]).astype(jnp.int32)
        d = lax.rem(mine - own[b] + traces, traces)

        @pl.when(d == 0)
        def _(b=b, here=here):
            start = pl.multiple_of(owner[mine, b] % blocks * rows, rows)
            pltpu.make_async_copy(pool.at[pl.ds(start, rows)], here, sem.at[b]).start()

        for far in range(1, traces):
            for nth in range(CAP):

                @pl.when((d == far) & (rank == nth))
                def _(b=b, here=here, block=slots[far][nth]):
                    pltpu.make_async_copy(block, here, sem.at[b]).start()

    width = kv.shape[1]
    n_q = fresh.shape[0]
    ones = jnp.ones((n_q, HD), BF)
    for b in range(blocks):
        here = pl.ds(b * rows, rows)
        at = lax.broadcasted_iota(jnp.int32, (rows, n_q), 0) + b * rows
        hits = (at == spots[...]).astype(F32).astype(BF)
        chosen = jnp.dot(hits, ones, preferred_element_type=F32) > 0.5
        pltpu.make_async_copy(two_up.at[0], kv.at[here], sem.at[b]).wait()
        cos, sin = kcos[b : b + 1, :], ksin[b : b + 1, :]
        for n in range(width // HD):
            cols = pl.ds(n * HD, HD)
            x = kv[here, cols]
            x = rotated(x, cos, sin) if n < KH else x.astype(F32)
            placed = jnp.dot(hits, fresh[:, cols], preferred_element_type=F32)
            kv[here, cols] = jnp.where(chosen, placed, x).astype(BF)
        pltpu.make_async_copy(kv.at[here], blended.at[here], out_sem.at[b]).start()
    for b in range(blocks):
        here = pl.ds(b * rows, rows)
        pltpu.make_async_copy(kv.at[here], blended.at[here], out_sem.at[b]).wait()


def own_kernel(q0, kv, num0, den0, stack):
    tokens = kv.shape[0]
    n_q = q0.shape[0]
    key = lax.broadcasted_iota(jnp.int32, (n_q, tokens), 1)

    def put(i, cols, num):
        num0[:, cols] = num

    (den0[...],) = attend([q0], kv, stack, [key <= token_of(q0, tokens)], put)


def remote_kernel(q1, q2, kv, p1, p2, stack):
    tokens = kv.shape[0]
    n_q = q1.shape[0]
    key = lax.broadcasted_iota(jnp.int32, (n_q, tokens), 1)

    def put(i, cols, num):
        (p1, p2)[i][:, cols] = num.astype(BF)

    sums = attend([q1, q2], kv, stack, [None, key > token_of(q2, tokens)], put)
    lane = lax.broadcasted_iota(jnp.int32, (n_q, HD), 1)
    for p, d in zip((p1, p2), sums):
        high = d.astype(BF)
        low = d - high.astype(F32)
        p[:, QH * HD :] = jnp.where(
            lane < QH, high.astype(F32), pltpu.roll(low, QH, 1)
        ).astype(BF)


def merge_kernel(num0, den0, r1, r2, live, out):
    total = den0[...]
    for r in (r1, r2):
        d = r[:, QH * HD :].astype(F32)
        total = total + d + pltpu.roll(d, HD - QH, 1)
    alive = live[...] > 0
    for h in range(QH):
        cols = pl.ds(h * HD, HD)
        num = num0[:, cols] + r1[:, cols].astype(F32) + r2[:, cols].astype(F32)
        out[:, cols] = jnp.where(alive, num / total[:, h : h + 1], 0.0).astype(BF)


def half_turns(angles):
    cos, sin = jnp.cos(angles), jnp.sin(angles)
    return jnp.concatenate([cos, cos], -1), jnp.concatenate([-sin, sin], -1)


def on_device(sel_hidden, w_qkv, cache_pool, block_owner, doc_lengths, sel_index, sel_count):
    ny, nz = lax.axis_size("y"), lax.axis_size("z")
    y = lax.axis_index("y")
    shard = lax.axis_index(SEQ)
    group = NX * NC
    n_seq = nz * group
    _, blocks, slots, d = sel_hidden.shape
    rows = blocks * slots
    tokens, kvw = cache_pool.shape[1:]
    block_len = tokens // blocks
    cols = w_qkv.shape[1]
    me = y.reshape(1).astype(jnp.int32)

    def turned(array, by):
        return lax.ppermute(array, "y", [(i, (i + by) % ny) for i in range(ny)])

    def room(n):
        return pltpu.HBM((n, block_len, kvw), BF)

    one_up, one_down, two_up, two_down, three_up, three_down = call(
        pick_kernel,
        (room(3), room(3), room(2), room(2), room(3), room(3)),
        [SM, SM, ANY], (ANY,) * 6,
        [
            pltpu.SMEM((blocks,), jnp.int32),
            pltpu.VMEM((tokens, kvw), BF),
            pltpu.SemaphoreType.DMA((blocks,)),
            pltpu.SemaphoreType.DMA((blocks,)),
        ],
        moved=4 * tokens * kvw,
    )(block_owner, me, *kept(cache_pool[0]))
    one_up, w_qkv = lax.optimization_barrier((one_up, w_qkv))
    one_up, one_down = turned(one_up, 1), turned(one_down, -1)

    def crossed(m):
        pairs = [(a * group + b, (b ^ m) * group + a) for a in range(ny) for b in range(group)]
        return lax.ppermute(w_qkv, ("y", "x", "c"), pairs)

    def paired(mine, other, bit, axis):
        low = (y // bit) % 2 == 0
        return jnp.stack([jnp.where(low, mine, other), jnp.where(low, other, mine)], axis)

    w = paired(
        paired(crossed(0), crossed(4), 4, 0), paired(crossed(2), crossed(6), 4, 0), 2, 1
    )
    w, one_up, one_down = lax.optimization_barrier((w, one_up, one_down))
    w = paired(w, lax.ppermute(w, "y", [(i, i ^ 1) for i in range(ny)]), 1, 2).reshape(-1, cols)
    w, two_up, two_down, one_up, one_down = lax.optimization_barrier(
        (w, two_up, two_down, one_up, one_down)
    )
    two_up, two_down = turned(two_up, 2), turned(two_down, -2)
    hidden = lax.all_gather(sel_hidden.reshape(rows, d), XC, axis=0, tiled=True)
    w, hidden = lax.optimization_barrier((w, hidden))
    w = lax.all_gather(w, "z", axis=0, tiled=True)
    three_up = turned(lax.dynamic_update_slice(three_up, one_up[2:], (2, 0, 0)), 3)
    three_down = turned(lax.dynamic_update_slice(three_down, one_down[2:], (2, 0, 0)), -3)
    hidden, w, two_up, two_down = lax.optimization_barrier((hidden, w, two_up, two_down))
    projected = jnp.dot(hidden, w, preferred_element_type=F32).astype(BF)
    projected = projected.reshape(group, rows, cols)
    merged = lax.all_to_all(projected, XC, 0, 0, tiled=True)

    frequency = 1.0 / BASE ** (jnp.arange(HD // 2, dtype=F32) * 2.0 / HD)
    index = jnp.arange(blocks, dtype=jnp.int32)
    local = (index[:, None] * block_len + sel_index[0]).reshape(rows)
    live = (jnp.arange(slots, dtype=jnp.int32)[None, :] < sel_count[0][:, None]).reshape(rows)
    cos, sin = half_turns((shard * tokens + local).astype(F32)[:, None] * frequency)
    lengths = lax.dynamic_index_in_dim(doc_lengths, y, 0, keepdims=False)
    nth = jnp.arange(lengths.shape[0], dtype=jnp.int32)
    ends = jnp.sum(jnp.where(nth[None, :] <= nth[:, None], lengths[None, :], 0), axis=1)
    here = shard * blocks + index
    first = jnp.sum(jnp.where(ends[None, :] <= here[:, None], lengths[None, :], 0), axis=1)
    kcos, ksin = half_turns((first * block_len).astype(F32)[:, None] * frequency)
    spots = jnp.where(live, local, -1).reshape(1, rows)

    wide = QH * HD + HD
    queries, fresh = call(
        rope_kernel,
        (jax.ShapeDtypeStruct((rows, wide), BF), jax.ShapeDtypeStruct((rows, kvw), BF)),
        [VM] * 4, (VM, VM),
        moved=4 * rows * (wide + kvw),
    )(merged, cos, sin, sel_index.reshape(rows, 1))

    def along(array, by):
        pairs = [(i, i + by) for i in range(n_seq) if 0 <= i + by < n_seq]
        return lax.ppermute(array, SEQ, pairs)

    q1, q2 = along(queries, -1), along(queries, -2)
    blended, kv = call(
        blend_kernel,
        (jax.ShapeDtypeStruct((tokens, kvw), BF),) * 2,
        [SM, SM] + [VM] * 4 + [ANY] * 7, (ANY, VM),
        [pltpu.SemaphoreType.DMA((blocks,)), pltpu.SemaphoreType.DMA((blocks,))],
        moved=6 * tokens * kvw,
    )(
        block_owner, me, kcos, ksin, spots, fresh,
        *kept(cache_pool[0], one_up, one_down, two_up, two_down, three_up, three_down),
    )
    p1, p2 = call(
        remote_kernel,
        (jax.ShapeDtypeStruct((rows, wide), BF),) * 2,
        [VM] * 3, (VM, VM),
        [pltpu.VMEM((2, GROUP * rows, HD), BF)],
        flops=8 * rows * QH * HD * tokens,
        moved=2 * tokens * kvw,
        vmem=20,
    )(q1, q2, kv)
    whole, p1, p2 = lax.optimization_barrier((blended, p1, p2))
    r1, r2 = along(p1, 1), along(p2, 2)
    num0, den0 = call(
        own_kernel,
        (jax.ShapeDtypeStruct((rows, QH * HD), F32), jax.ShapeDtypeStruct((rows, HD), F32)),
        [VM] * 2, (VM, VM),
        [pltpu.VMEM((1, GROUP * rows, HD), BF)],
        flops=4 * rows * QH * HD * tokens,
        moved=2 * tokens * kvw,
        vmem=20,
    )(queries, whole)
    attended = call(
        merge_kernel,
        jax.ShapeDtypeStruct((rows, QH * HD), BF),
        [VM] * 5, VM,
        moved=12 * rows * QH * HD,
    )(num0, den0, r1, r2, live.astype(jnp.int32).reshape(rows, 1))
    return attended.reshape(1, blocks, slots, QH * HD), blended[None]


def solution(mesh):
    ny, n_seq = mesh.devices.shape
    fine = Mesh(
        mesh.devices.reshape(ny, n_seq // (NX * NC), NX, NC), ("y", "z", "x", "c")
    )
    return jax.shard_map(
        on_device,
        mesh=fine,
        in_specs=(
            P("y", SEQ, None, None),
            P(SEQ, "y"),
            P("y", SEQ, None),
            P(None, SEQ),
            P(),
            P("y", SEQ, None),
            P("y", SEQ),
        ),
        out_specs=(P("y", SEQ, None, None), P("y", SEQ, None)),
        check_vma=False,
    )
```
